256 devices in a mesh: group: 8 (over x_lo, y), fsdp: 32 (over x_hi, z, core).
Axes of the slice: x: 4 (x_hi: 2, x_lo: 2; x = x_hi * 2 + x_lo), y: 4, z: 8, core: 2. Of those that a mesh axis runs over, the one named last changes fastest.
Arguments:
- delta_codes: int32 [8, 8192, 512], P('group', 'fsdp'), may hold values from -32704 to 32704
- master_weights: float32 [8192, 512], P('fsdp'), may hold values from -6 to 6
- outer_momentum: float32 [8192, 512], P('fsdp'), may hold values from -3 to 3
- activations: bfloat16 [65536, 8192], P(('group', 'fsdp')), may hold values from -6 to 6
- key_cotangent: bfloat16 [65536, 512], P(('group', 'fsdp')), may hold values from -6 to 6
Outputs:
- new_weights: float32 [8192, 512], P('fsdp')
- new_momentum: float32 [8192, 512], P('fsdp')
- projected_keys: bfloat16 [65536, 512], P(('group', 'fsdp'))
- input_grads: bfloat16 [65536, 8192], P(('group', 'fsdp'))
- weight_grads: float32 [8, 8192, 512], P('group', 'fsdp')
The draws below stay inside these ranges and needn't reach their ends.
All inputs are finite; a program needn't handle non-finite values.
Results may differ from the reference program's by a relative error of at most 0.007.
Values may be sent and summed in bfloat16 or wider, within the bound.
A program may use at most 128 MiB of HBM per device.

```python
import jax
import jax.numpy as jnp
from jax import lax

D = 8192
KW = 512
TOK_DEV = 256
TOKENS = 65536
N_GROUP = 8
N_FSDP = 32


def draw_delta_codes(key, part):
    key = jax.random.fold_in(key, 7)
    blocks = KW // 128
    streams = jax.random.split(key, 5)
    block_shape = (N_GROUP, D, blocks, 1)
    exponent = jax.random.randint(streams[0], block_shape, 11, 15, dtype=jnp.int32)
    lowest = jnp.left_shift(jnp.ones_like(exponent), exponent)
    fraction = jax.random.randint(streams[1], block_shape, 0, 65536, dtype=jnp.int32)
    peak_code = jnp.minimum(lowest + fraction * lowest // 65536, 32704)
    row_index = lax.broadcasted_iota(jnp.int32, block_shape, 1)
    first_block = lax.broadcasted_iota(jnp.int32, block_shape, 2) == 0
    forced = first_block & (row_index < 2)
    peak_code = jnp.where(forced, 32704, peak_code)
    polarity = jax.random.randint(streams[2], block_shape, 0, 2, dtype=jnp.int32) * 2 - 1
    polarity = jnp.where(forced & (row_index == 0), 1, jnp.where(forced, -1, polarity))
    spread = peak_code // 42
    uniform = jax.random.randint(streams[3], (N_GROUP, D, blocks, 128), 0, 1048576, dtype=jnp.int32)
    small_codes = uniform * (2 * spread + 1) // 1048576 - spread
    outlier_lane = jax.random.randint(streams[4], block_shape, 0, 128, dtype=jnp.int32)
    lane_index = lax.broadcasted_iota(jnp.int32, small_codes.shape, 3)
    drawn_codes = jnp.where(lane_index == outlier_lane, polarity * peak_code, small_codes)
    return drawn_codes.reshape(N_GROUP, D, KW).astype(jnp.int32)


def shard_levels(own_key, shape, cuts, smallest, high):
    level = 1.0
    for axis_at, parts in cuts:
        heights = jax.random.uniform(jax.random.fold_in(jax.random.fold_in(own_key, 6), axis_at), (parts,), jnp.float32, smallest / len(cuts), high / len(cuts))
        level = level * jnp.repeat(jnp.exp(heights), shape[axis_at] // parts).reshape((-1,) + (1,) * (len(shape) - 1 - axis_at))
    return level


def scatter_about(own_key, shape, scale, bound, shards=(), kind=jnp.bfloat16):
    entries = jax.random.normal(own_key, shape, jnp.float32) * scale
    if len(shards) > 0:
        entries = shard_levels(own_key, shape, shards, -0.22, 0.18) * entries
    return jnp.clip(entries, min=-bound, max=bound).astype(kind)


def setup_inputs(seed: int = 0) -> dict:
    key_of = jax.random.split(jax.random.key(seed), 6)
    return {
        "delta_codes": draw_delta_codes(jax.random.fold_in(key_of[5], 71), 0),
        "master_weights": scatter_about(key_of[1], (D, KW), 1.0, 6.0, ((0, 32),), jnp.float32),
        "outer_momentum": scatter_about(key_of[2], (D, KW), 0.5, 3.0, ((0, 32),), jnp.float32),
        "activations": scatter_about(key_of[3], (TOKENS, D), 1.0, 6.0, ((0, 256),)),
        "key_cotangent": scatter_about(key_of[4], (TOKENS, KW), 1.0, 6.0, ((0, 256),)),
    }


unit_step = 1.0 / 4096.0


def dequantize(delta_codes):
    blocks = delta_codes.reshape(delta_codes.shape[:-1] + (delta_codes.shape[-1] // 128, 128))
    largest = jnp.max(jnp.abs(blocks), axis=-1, keepdims=True)
    block_scale = largest // 127 + 1
    magnitude = (jnp.abs(blocks) + block_scale // 2) // block_scale
    quantized = jnp.sign(blocks) * magnitude
    values = (quantized * block_scale).astype(jnp.float32) * unit_step
    return values.reshape(delta_codes.shape)


def reference(delta_codes, master_weights, outer_momentum, activations, key_cotangent):
    dequantized = dequantize(delta_codes)
    outer_grad = jnp.sum(dequantized, axis=0) / N_GROUP
    new_momentum = 0.9 * outer_momentum + outer_grad
    new_weights = master_weights - 0.7 * (outer_grad + 0.9 * new_momentum)
    inner_weights = new_weights.astype(jnp.bfloat16)
    scale = D ** -0.5
    group_inputs = activations.reshape(N_GROUP, N_FSDP * TOK_DEV, D)
    group_cots = key_cotangent.reshape(N_GROUP, N_FSDP * TOK_DEV, KW)

    def one_group(pair):
        inputs, cots = pair
        keys = (jnp.dot(inputs, inner_weights, preferred_element_type=jnp.float32) * scale).astype(jnp.bfloat16)
        grads_in = lax.dot_general(cots, inner_weights, (((1,), (1,)), ((), ())), preferred_element_type=jnp.float32)
        grads_in = (grads_in * scale).astype(jnp.bfloat16)
        grads_w = lax.dot_general(inputs, cots, (((0,), (0,)), ((), ())), preferred_element_type=jnp.float32) * scale
        return keys, grads_in, grads_w

    keys, grads_in, grads_w = lax.map(one_group, (group_inputs, group_cots))
    return (new_weights, new_momentum, keys.reshape(-1, KW), grads_in.reshape(-1, D), grads_w)
```

```python
import functools

import jax
import jax.numpy as jnp
from jax import lax
from jax.experimental import pallas as pl
from jax.experimental.pallas import tpu as pltpu
from jax.sharding import PartitionSpec as P

MESH = pl.DeviceIdType.MESH
F32 = jnp.float32
BF16 = jnp.bfloat16
NX, NY, NZ = 4, 4, 8
GROUPS = 8


def device(x, y, z, c):
    return (lax.rem(x, 2) * 4 + y, lax.div(x, 2) * 16 + z * 2 + c)


def up(v, d, n):
    return lax.rem(v + d, n)


def dequantize(codes):
    values = codes.astype(F32)
    size = jnp.abs(values)
    largest = jnp.max(size, axis=-1, keepdims=True)
    scale = jnp.floor((largest + 0.5) / 127.0) + 1.0
    half = jnp.floor(scale * 0.5)
    magnitude = jnp.floor((size + half + 0.5) / scale)
    signed = jnp.where(values < 0.0, -magnitude, magnitude)
    return signed * scale * (1.0 / 4096.0)


def nesterov(total, weights, momentum):
    outer_grad = total.astype(F32) / GROUPS
    moved = 0.9 * momentum + outer_grad
    return weights - 0.7 * (outer_grad + 0.9 * moved), moved


def kernel(
    delta_hbm, master_hbm, momentum_hbm, acts_hbm, cot_hbm,
    weights_out, moved_out, keys_out, grads_hbm, wgrad_out,
    delta, master, momentum, cot, cot_t, acts,
    coded, coded_in, total, gathered,
    chain_out, chain_in, cross_out, cross_in, cross_own,
    keys, keys_in, back,
    load_sem, acts_load, acts_send, acts_recv, pair_send, pair_recv,
    coded_send, coded_recv, total_send, total_recv,
    z_send, z_recv, x_send, x_recv, y_send, y_recv, f_send, f_recv,
    chain_send, chain_recv, cross_send, cross_recv,
    back_store, back_send, back_recv,
):
    tokens, width = acts_hbm.shape
    kw = cot_hbm.shape[1]
    block = width // 32
    piece = block // GROUPS
    half = kw // 2
    out_scale = width ** (-0.5)

    g, f = lax.axis_index("group"), lax.axis_index("fsdp")
    y, x_lo = lax.rem(g, NY), lax.div(g, NY)
    c, z, x_hi = lax.rem(f, 2), lax.rem(lax.div(f, 2), NZ), lax.div(f, 16)
    x = 2 * x_hi + x_lo
    other = 1 - c
    sibling = device(x, y, z, other)

    def member(j):
        return device(2 * x_hi + lax.div(j, NY), lax.rem(j, NY), z, c)

    def remote(src, dst, send, recv, to):
        return pltpu.make_async_remote_copy(
            src_ref=src, dst_ref=dst, send_sem=send, recv_sem=recv, device_id=to, device_id_type=MESH
        )

    def columns(hi, zz, core):
        return pl.ds(pl.multiple_of((hi * 16 + zz * 2 + core) * block, block), block)

    def tokens_of(core):
        return pl.ds(pl.multiple_of(core * tokens, tokens), tokens)

    loads = [
        pltpu.make_async_copy(delta_hbm, delta, load_sem.at[0]),
        pltpu.make_async_copy(cot_hbm, cot.at[tokens_of(c)], load_sem.at[1]),
        pltpu.make_async_copy(master_hbm, master, load_sem.at[2]),
        pltpu.make_async_copy(momentum_hbm, momentum, load_sem.at[3]),
    ]
    for load in loads:
        load.start()

    def act_load(zz, hi):
        return pltpu.make_async_copy(
            acts_hbm.at[:, columns(hi, zz, c)], acts.at[zz, hi, tokens_of(c)], acts_load.at[zz, hi]
        )

    def act_swap(zz, hi):
        return remote(
            acts_hbm.at[:, columns(hi, zz, other)], acts.at[zz, hi, tokens_of(c)],
            acts_send.at[zz, hi], acts_recv.at[zz, hi], sibling,
        )

    def act_arrived(zz, hi):
        return remote(
            acts_hbm.at[:, columns(hi, zz, other)], acts.at[zz, hi, tokens_of(other)],
            acts_send.at[zz, hi], acts_recv.at[zz, hi], sibling,
        )

    def far(i):
        step = lax.div(i + 1, 2)
        return lax.rem(z + 4 + step * (2 * lax.rem(i, 2) - 1) * -1 + NZ, NZ)

    @pl.loop(0, NZ)
    def _(i):
        for hi in range(2):
            act_load(far(i), hi).start()

    partners = [sibling]
    partners += [device(x, y, up(z, d, NZ), c) for d in range(1, NZ)]
    partners += [device(up(x, d, NX), y, z, c) for d in range(1, NX)]
    partners += [device(x, up(y, d, NY), z, c) for d in range(1, NY)]
    partners += [device(2 * x_hi + 1 - x_lo, up(y, d, NY), z, c) for d in range(1, NY)]
    barrier = pltpu.get_barrier_semaphore()
    for partner in partners:
        pl.semaphore_signal(barrier, inc=1, device_id=partner, device_id_type=MESH)
    pl.semaphore_wait(barrier, len(partners))

    cot_swap = remote(cot_hbm, cot.at[tokens_of(c)], pair_send.at[0], pair_recv.at[0], sibling)
    cot_swap.start()

    @pl.loop(0, NZ)
    def _(i):
        for hi in range(2):
            act_swap(far(i), hi).start()

    loads[0].wait()
    for j in range(GROUPS):
        for k in range(kw // 128):
            codes = delta[pl.ds(j * piece, piece), pl.ds(k * 128, 128)]
            coded[j, :, pl.ds(k * 128, 128)] = dequantize(codes).astype(BF16)

    def coded_copy(d):
        j = up(g, d, GROUPS)
        return remote(coded.at[j], coded_in.at[g], coded_send.at[d], coded_recv.at[g], member(j))

    def coded_arrived(j):
        return remote(coded.at[j], coded_in.at[j], coded_send.at[0], coded_recv.at[j], sibling)

    @pl.loop(1, GROUPS)
    def _(d):
        coded_copy(d).start()

    loads[1].wait()
    remote(cot_hbm, cot.at[tokens_of(other)], pair_send.at[0], pair_recv.at[0], sibling).wait_recv()
    cot_t[...] = cot[...].T.reshape(2, half, 2 * tokens)

    def acts_ready(zz):
        for hi in range(2):
            act_load(zz, hi).wait()
            act_arrived(zz, hi).wait_recv()

    def chain_copy(way, k):
        to = device(x, y, up(z, 1 if way == 0 else NZ - 1, NZ), c)
        return remote(
            chain_out.at[way, k], chain_in.at[way, k], chain_send.at[way, k], chain_recv.at[way, k], to
        )

    def share(h, zz, hi):
        return jnp.dot(cot_t[h], acts[zz, hi], preferred_element_type=F32)

    def chain(k, first):
        s = lax.div(k + 1, 2)
        for way in range(2):
            zz = up(z, 4 - s if way == 0 else 4 + s, NZ)
            h = lax.rem(k + way, 2)
            if not first:
                chain_copy(way, k - 2).wait_recv()
            for hi in range(2):
                sent = share(h, zz, hi)
                if not first:
                    sent += chain_in[way, k - 2, hi].astype(F32)
                chain_out[way, k, hi] = sent.astype(BF16)
            chain_copy(way, k).start()

    acts_ready(far(0))
    chain(0, True)

    rows = pl.ds(pl.multiple_of(g * piece, piece), piece)

    @pl.loop(1, GROUPS)
    def _(d):
        coded_arrived(up(g, d, GROUPS)).wait_recv()

    summed = coded[g].astype(F32)
    for d in range(1, GROUPS):
        summed += coded_in[up(g, d, GROUPS)].astype(F32)
    total[g] = summed.astype(BF16)
    loads[2].wait()
    loads[3].wait()
    updated, _ = nesterov(total[g], master[rows, :], momentum[rows, :])
    gathered[z, y, x] = updated.astype(BF16)

    def z_copy(d):
        return remote(
            gathered.at[z, y, x], gathered.at[z, y, x], z_send.at[d], z_recv.at[z],
            device(x, y, up(z, d, NZ), c),
        )

    def z_arrived(zz):
        return remote(gathered.at[zz, y, x], gathered.at[zz, y, x], z_send.at[0], z_recv.at[zz], sibling)

    def x_copy(zz, d):
        return remote(
            gathered.at[zz, y, x], gathered.at[zz, y, x], x_send.at[zz, d], x_recv.at[zz, x],
            device(up(x, d, NX), y, z, c),
        )

    def x_arrived(zz, xx):
        return remote(
            gathered.at[zz, y, xx], gathered.at[zz, y, xx], x_send.at[zz, 0], x_recv.at[zz, xx], sibling
        )

    def y_copy(zz, way):
        to = device(x, up(y, 1 if way == 0 else NY - 1, NY), z, c)
        return remote(gathered.at[zz, y], gathered.at[zz, y], y_send.at[zz, way], y_recv.at[zz, way], to)

    def y_arrived(zz, way):
        yy = up(y, NY - 1 if way == 0 else 1, NY)
        return remote(
            gathered.at[zz, yy], gathered.at[zz, yy], y_send.at[zz, way], y_recv.at[zz, way], sibling
        )

    def f_copy(zz, way):
        yy = up(y, NY - 1 if way == 0 else 1, NY)
        to = device(x, up(y, 1 if way == 0 else NY - 1, NY), z, c)
        part = gathered.at[zz, yy, pl.ds(way * 2, 2)]
        return remote(part, part, f_send.at[zz, way], f_recv.at[zz, way], to)

    def f_arrived(zz, way):
        part = gathered.at[zz, up(y, 2, NY), pl.ds(way * 2, 2)]
        return remote(part, part, f_send.at[zz, way], f_recv.at[zz, way], sibling)

    for d in (1, 7, 2, 6, 3, 5, 4):
        z_copy(d).start()
    for d in range(1, NX):
        x_copy(z, d).start()

    def total_copy(d):
        return remote(
            total.at[g], total.at[g], total_send.at[d], total_recv.at[g], member(up(g, d, GROUPS))
        )

    def total_arrived(j):
        return remote(total.at[j], total.at[j], total_send.at[0], total_recv.at[j], sibling)

    @pl.loop(1, GROUPS)
    def _(d):
        total_copy(d).start()

    acts_ready(far(1))
    acts_ready(far(2))
    chain(1, True)

    @pl.loop(3, NZ)
    def _(i):
        acts_ready(far(i))

    def wave(i):
        return lax.rem(z + lax.div(i + 1, 2) * (2 * lax.rem(i, 2) - 1) + NZ, NZ)

    keys[...] = jnp.zeros_like(keys)

    def back_local(zz, hi):
        return pltpu.make_async_copy(
            back.at[zz, hi, tokens_of(c)], grads_hbm.at[:, columns(hi, zz, c)], back_store.at[zz, hi]
        )

    def back_copy(zz, hi):
        return remote(
            back.at[zz, hi, tokens_of(other)], grads_hbm.at[:, columns(hi, zz, c)],
            back_send.at[zz, hi], back_recv.at[zz, hi], sibling,
        )

    def back_arrived(zz, hi):
        return remote(
            back.at[zz, hi, tokens_of(other)], grads_hbm.at[:, columns(hi, zz, other)],
            back_send.at[zz, hi], back_recv.at[zz, hi], sibling,
        )

    def multiply(zz):
        for hi in range(2):
            lower = [gathered[zz, :, 2 * hi + lo].reshape(block // 2, kw) for lo in range(2)]
            w = jnp.concatenate(lower, axis=0)
            grads = lax.dot_general(cot[...], w, (((1,), (1,)), ((), ())), preferred_element_type=F32)
            back[zz, hi] = (grads * out_scale).astype(BF16)
            back_copy(zz, hi).start()
            back_local(zz, hi).start()
            keys[...] += jnp.dot(acts[zz, hi], w, preferred_element_type=F32)

    def cross_copy(h):
        return remote(
            cross_out.at[h], cross_in.at[h], cross_send.at[h], cross_recv.at[h], device(up(x, 2, NX), y, z, c)
        )

    def chain_end():
        for way in range(2):
            for k in (5, 6):
                chain_copy(way, k).wait_recv()
        for mine in range(2):
            hi = x_hi if mine else 1 - x_hi
            for h in range(2):
                done = share(h, z, hi) + chain_in[0, 6 - h, hi].astype(F32) + chain_in[1, 5 + h, hi].astype(F32)
                if mine:
                    cross_own[h] = done
                else:
                    cross_out[h] = done.astype(BF16)
                    cross_copy(h).start()

    @pl.loop(1, NZ + 3)
    def _(i):
        @pl.when(i < NZ)
        def _():
            zz = wave(i)
            z_arrived(zz).wait_recv()
            for d in range(1, NX):
                x_copy(zz, d).start()

        @pl.when(i < NZ + 1)
        def _():
            zz = wave(i - 1)
            for d in range(1, NX):
                x_arrived(zz, up(x, d, NX)).wait_recv()
            for way in range(2):
                y_copy(zz, way).start()

        @pl.when(jnp.logical_and(i >= 2, i < NZ + 2))
        def _():
            zz = wave(i - 2)
            for way in range(2):
                y_arrived(zz, way).wait_recv()
            for way in range(2):
                f_copy(zz, way).start()

        @pl.when(i < 6)
        def _():
            chain(i + 1, False)

        @pl.when(i == 7)
        def _():
            chain_end()

        @pl.when(i >= 3)
        def _():
            zz = wave(i - 3)
            for way in range(2):
                f_arrived(zz, way).wait_recv()
            multiply(zz)

    keys_copy = remote(keys.at[tokens_of(other)], keys_in, pair_send.at[1], pair_recv.at[1], sibling)
    keys_copy.start()

    for j in range(GROUPS):
        @pl.when(g != j)
        def _():
            total_arrived(j).wait_recv()

    for j in range(GROUPS):
        own = pl.ds(j * piece, piece)
        weights_out[own, :], moved_out[own, :] = nesterov(total[j], master[own, :], momentum[own, :])

    for h in range(2):
        cross_copy(h).wait_recv()
        wgrad_out[pl.ds(h * half, half), :] = (cross_own[h] + cross_in[h].astype(F32)) * out_scale

    keys_copy.wait_recv()
    keys_out[...] = ((keys[tokens_of(c), :] + keys_in[...]) * out_scale).astype(BF16)

    cot_swap.wait_send()
    keys_copy.wait_send()
    for h in range(2):
        cross_copy(h).wait_send()

    @pl.loop(0, NZ)
    def _(zz):
        for hi in range(2):
            act_swap(zz, hi).wait_send()
            back_local(zz, hi).wait()
            back_copy(zz, hi).wait_send()
            back_arrived(zz, hi).wait_recv()
        for d in range(1, NX):
            x_copy(zz, d).wait_send()
        for way in range(2):
            y_copy(zz, way).wait_send()
            f_copy(zz, way).wait_send()

    @pl.loop(1, NZ)
    def _(d):
        coded_copy(d).wait_send()
        total_copy(d).wait_send()
        z_copy(d).wait_send()
        for way in range(2):
            chain_copy(way, d - 1).wait_send()


def body(delta_codes, master_weights, outer_momentum, activations, key_cotangent):
    tokens, width = activations.shape
    rows, kw = master_weights.shape
    block, piece, half = width // 32, width // 32 // GROUPS, kw // 2
    dma = pltpu.SemaphoreType.DMA
    hbm = pl.BlockSpec(memory_space=pl.ANY)
    vmem = pl.BlockSpec(memory_space=pltpu.VMEM)
    weights, moved, keys, grads, wgrad = pl.pallas_call(
        kernel,
        name="outer_step",
        out_shape=(
            jax.ShapeDtypeStruct((rows, kw), F32),
            jax.ShapeDtypeStruct((rows, kw), F32),
            jax.ShapeDtypeStruct((tokens, kw), BF16),
            jax.ShapeDtypeStruct((tokens, width), BF16),
            jax.ShapeDtypeStruct((kw, block), F32),
        ),
        in_specs=[hbm] * 5,
        out_specs=(vmem, vmem, vmem, hbm, vmem),
        scratch_shapes=[
            pltpu.VMEM((rows, kw), jnp.int32),
            pltpu.VMEM((rows, kw), F32),
            pltpu.VMEM((rows, kw), F32),
            pltpu.VMEM((2 * tokens, kw), BF16),
            pltpu.VMEM((2, half, 2 * tokens), BF16),
            pltpu.VMEM((NZ, 2, 2 * tokens, block), BF16),
            pltpu.VMEM((GROUPS, piece, kw), BF16),
            pltpu.VMEM((GROUPS, piece, kw), BF16),
            pltpu.VMEM((GROUPS, piece, kw), BF16),
            pltpu.VMEM((NZ, NY, NX, piece, kw), BF16),
            pltpu.VMEM((2, 7, 2, half, block), BF16),
            pltpu.VMEM((2, 7, 2, half, block), BF16),
            pltpu.VMEM((2, half, block), BF16),
            pltpu.VMEM((2, half, block), BF16),
            pltpu.VMEM((2, half, block), F32),
            pltpu.VMEM((2 * tokens, kw), F32),
            pltpu.VMEM((tokens, kw), F32),
            pltpu.VMEM((NZ, 2, 2 * tokens, block), BF16),
            dma((4,)),
            dma((NZ, 2)),
            dma((NZ, 2)),
            dma((NZ, 2)),
            dma((2,)),
            dma((2,)),
            dma((GROUPS,)),
            dma((GROUPS,)),
            dma((GROUPS,)),
            dma((GROUPS,)),
            dma((NZ,)),
            dma((NZ,)),
            dma((NZ, NX)),
            dma((NZ, NX)),
            dma((NZ, 2)),
            dma((NZ, 2)),
            dma((NZ, 2)),
            dma((NZ, 2)),
            dma((2, 7)),
            dma((2, 7)),
            dma((2,)),
            dma((2,)),
            dma((NZ, 2)),
            dma((NZ, 2)),
            dma((NZ, 2)),
        ],
        compiler_params=pltpu.CompilerParams(
            collective_id=0, has_side_effects=True, vmem_limit_bytes=52 * 2**20
        ),
        cost_estimate=pl.CostEstimate(
            flops=6 * tokens * width * kw, bytes_accessed=16 * 2**20, transcendentals=0
        ),
    )(delta_codes[0], master_weights, outer_momentum, activations, key_cotangent)
    return weights, moved, keys, grads, wgrad.T[None]


def solution(mesh):
    placed = (
        P("group", "fsdp", None),
        P("fsdp", None),
        P("fsdp", None),
        P(("group", "fsdp"), None),
        P(("group", "fsdp"), None),
    )
    return jax.shard_map(
        body,
        mesh=mesh,
        in_specs=placed,
        out_specs=(
            P("fsdp", None),
            P("fsdp", None),
            P(("group", "fsdp"), None),
            P(("group", "fsdp"), None),
            P("group", "fsdp", None),
        ),
        check_vma=False,
    )
```

```python
import functools

import jax
import jax.numpy as jnp
from jax import lax
from jax.experimental import pallas as pl
from jax.experimental.pallas import tpu as pltpu
from jax.sharding import PartitionSpec as P

MESH = pl.DeviceIdType.MESH
F32 = jnp.float32
BF16 = jnp.bfloat16
NX, NY, NZ = 4, 4, 8
GROUPS = 8
LAG_Y, LAG_F, LAG_END = 1, 3, 5


def device(x, y, z, c):
    return (lax.rem(x, 2) * 4 + y, lax.div(x, 2) * 16 + z * 2 + c)


def up(v, d, n):
    return lax.rem(v + d, n)


def dequantize(codes):
    values = codes.astype(F32)
    size = jnp.abs(values)
    largest = jnp.max(size, axis=-1, keepdims=True)
    scale = jnp.floor((largest + 0.5) / 127.0) + 1.0
    half = jnp.floor(scale * 0.5)
    magnitude = jnp.floor((size + half + 0.5) / scale)
    signed = jnp.where(values < 0.0, -magnitude, magnitude)
    return signed * scale * (1.0 / 4096.0)


def nesterov(total, weights, momentum):
    outer_grad = total.astype(F32) / GROUPS
    moved = 0.9 * momentum + outer_grad
    return weights - 0.7 * (outer_grad + 0.9 * moved), moved


def kernel(
    delta_hbm, master_hbm, momentum_hbm, acts_hbm, cot_hbm,
    weights_out, moved_out, keys_out, grads, wgrad_out,
    delta, master, momentum, cot, cot_t, acts,
    coded, coded_in, total, gathered,
    chain_out, chain_in, cross_out, cross_in, cross_own,
    keys, keys_in, back,
    load_sem, acts_load, acts_send, acts_recv, pair_send, pair_recv,
    coded_send, coded_recv, total_send, total_recv,
    z_send, z_recv, x_send, x_recv, y_send, y_recv, f_send, f_recv,
    chain_send, chain_recv, cross_send, cross_recv,
    back_send, back_recv,
):
    tokens, width = acts_hbm.shape
    kw = cot_hbm.shape[1]
    block = width // 32
    piece = block // GROUPS
    half = kw // 2
    out_scale = width ** (-0.5)

    g, f = lax.axis_index("group"), lax.axis_index("fsdp")
    y, x_lo = lax.rem(g, NY), lax.div(g, NY)
    c, z, x_hi = lax.rem(f, 2), lax.rem(lax.div(f, 2), NZ), lax.div(f, 16)
    x = 2 * x_hi + x_lo
    other = 1 - c
    sibling = device(x, y, z, other)

    def member(j):
        return device(2 * x_hi + lax.div(j, NY), lax.rem(j, NY), z, c)

    def remote(src, dst, send, recv, to):
        return pltpu.make_async_remote_copy(
            src_ref=src, dst_ref=dst, send_sem=send, recv_sem=recv, device_id=to, device_id_type=MESH
        )

    def columns(hi, zz, core):
        return pl.ds(pl.multiple_of((hi * 16 + zz * 2 + core) * block, block), block)

    def tokens_of(core):
        return pl.ds(pl.multiple_of(core * tokens, tokens), tokens)

    loads = [
        pltpu.make_async_copy(delta_hbm, delta, load_sem.at[0]),
        pltpu.make_async_copy(cot_hbm, cot.at[tokens_of(c)], load_sem.at[1]),
        pltpu.make_async_copy(master_hbm, master, load_sem.at[2]),
        pltpu.make_async_copy(momentum_hbm, momentum, load_sem.at[3]),
    ]
    for load in loads:
        load.start()

    def act_load(zz, hi):
        return pltpu.make_async_copy(
            acts_hbm.at[:, columns(hi, zz, c)], acts.at[zz, hi, tokens_of(c)], acts_load.at[zz, hi]
        )

    def act_swap(zz, hi):
        return remote(
            acts_hbm.at[:, columns(hi, zz, other)], acts.at[zz, hi, tokens_of(c)],
            acts_send.at[zz, hi], acts_recv.at[zz, hi], sibling,
        )

    def act_arrived(zz, hi):
        return remote(
            acts_hbm.at[:, columns(hi, zz, other)], acts.at[zz, hi, tokens_of(other)],
            acts_send.at[zz, hi], acts_recv.at[zz, hi], sibling,
        )

    def far(i):
        step = lax.div(i + 1, 2)
        return lax.rem(z + 4 + step * (2 * lax.rem(i, 2) - 1) * -1 + NZ, NZ)

    @pl.loop(0, NZ)
    def _(i):
        for hi in range(2):
            act_load(far(i), hi).start()

    partners = [sibling]
    partners += [device(x, y, up(z, d, NZ), c) for d in range(1, NZ)]
    partners += [device(up(x, d, NX), y, z, c) for d in range(1, NX)]
    partners += [device(x, up(y, d, NY), z, c) for d in range(1, NY)]
    partners += [device(2 * x_hi + 1 - x_lo, up(y, d, NY), z, c) for d in range(1, NY)]
    barrier = pltpu.get_barrier_semaphore()
    for partner in partners:
        pl.semaphore_signal(barrier, inc=1, device_id=partner, device_id_type=MESH)

    loads[0].wait()
    for j in range(GROUPS):
        for k in range(kw // 128):
            codes = delta[pl.ds(j * piece, piece), pl.ds(k * 128, 128)]
            coded[j, :, pl.ds(k * 128, 128)] = dequantize(codes).astype(BF16)
    loads[1].wait()
    cot_t[c] = cot[tokens_of(c), :].T.reshape(2, half, tokens)
    pl.semaphore_wait(barrier, len(partners))

    def coded_copy(d):
        j = up(g, d, GROUPS)
        return remote(coded.at[j], coded_in.at[g], coded_send.at[d], coded_recv.at[g], member(j))

    def coded_arrived(j):
        return remote(coded.at[j], coded_in.at[j], coded_send.at[0], coded_recv.at[j], sibling)

    @pl.loop(1, GROUPS)
    def _(d):
        coded_copy(d).start()

    cot_swap = remote(cot_hbm, cot.at[tokens_of(c)], pair_send.at[0], pair_recv.at[0], sibling)
    cot_swap.start()
    cot_t_swap = remote(cot_t.at[c], cot_t.at[c], pair_send.at[2], pair_recv.at[2], sibling)
    cot_t_swap.start()

    @pl.loop(0, NZ)
    def _(i):
        for hi in range(2):
            act_swap(far(i), hi).start()


    def acts_ready(zz):
        for hi in range(2):
            act_load(zz, hi).wait()
            act_arrived(zz, hi).wait_recv()

    def chain_copy(way, k):
        to = device(x, y, up(z, 1 if way == 0 else NZ - 1, NZ), c)
        return remote(
            chain_out.at[way, k], chain_in.at[way, k], chain_send.at[way, k], chain_recv.at[way, k], to
        )

    def share(h, zz, hi):
        turned = jnp.concatenate([cot_t[0, h], cot_t[1, h]], axis=1)
        return jnp.dot(turned, acts[zz, hi], preferred_element_type=F32)

    def chain(k, first):
        s = lax.div(k + 1, 2)
        for way in range(2):
            zz = up(z, 4 - s if way == 0 else 4 + s, NZ)
            h = lax.rem(k + way, 2)
            if not first:
                chain_copy(way, k - 2).wait_recv()
            for hi in range(2):
                sent = share(h, zz, hi)
                if not first:
                    sent += chain_in[way, k - 2, hi].astype(F32)
                chain_out[way, k, hi] = sent.astype(BF16)
            chain_copy(way, k).start()

    remote(cot_t.at[other], cot_t.at[other], pair_send.at[2], pair_recv.at[2], sibling).wait_recv()
    acts_ready(far(0))
    chain(0, True)

    rows = pl.ds(pl.multiple_of(g * piece, piece), piece)

    @pl.loop(1, GROUPS)
    def _(d):
        coded_arrived(up(g, d, GROUPS)).wait_recv()

    summed = coded[g].astype(F32)
    for d in range(1, GROUPS):
        summed += coded_in[up(g, d, GROUPS)].astype(F32)
    total[g] = summed.astype(BF16)
    loads[2].wait()
    loads[3].wait()
    updated, _ = nesterov(total[g], master[rows, :], momentum[rows, :])
    gathered[z, y, x] = updated.astype(BF16)

    def z_copy(d):
        return remote(
            gathered.at[z, y, x], gathered.at[z, y, x], z_send.at[d], z_recv.at[z],
            device(x, y, up(z, d, NZ), c),
        )

    def z_arrived(zz):
        return remote(gathered.at[zz, y, x], gathered.at[zz, y, x], z_send.at[0], z_recv.at[zz], sibling)

    def x_copy(zz, d):
        return remote(
            gathered.at[zz, y, x], gathered.at[zz, y, x], x_send.at[zz, d], x_recv.at[zz, x],
            device(up(x, d, NX), y, z, c),
        )

    def x_arrived(zz, xx):
        return remote(
            gathered.at[zz, y, xx], gathered.at[zz, y, xx], x_send.at[zz, 0], x_recv.at[zz, xx], sibling
        )

    def y_copy(zz, way):
        to = device(x, up(y, 1 if way == 0 else NY - 1, NY), z, c)
        return remote(gathered.at[zz, y], gathered.at[zz, y], y_send.at[zz, way], y_recv.at[zz, way], to)

    def y_arrived(zz, way):
        yy = up(y, NY - 1 if way == 0 else 1, NY)
        return remote(
            gathered.at[zz, yy], gathered.at[zz, yy], y_send.at[zz, way], y_recv.at[zz, way], sibling
        )

    def f_copy(zz, way):
        yy = up(y, NY - 1 if way == 0 else 1, NY)
        to = device(x, up(y, 1 if way == 0 else NY - 1, NY), z, c)
        part = gathered.at[zz, yy, pl.ds(way * 2, 2)]
        return remote(part, part, f_send.at[zz, way], f_recv.at[zz, way], to)

    def f_arrived(zz, way):
        part = gathered.at[zz, up(y, 2, NY), pl.ds(way * 2, 2)]
        return remote(part, part, f_send.at[zz, way], f_recv.at[zz, way], sibling)

    for d in (1, 7, 2, 6, 3, 5, 4):
        z_copy(d).start()
    for d in range(1, NX):
        x_copy(z, d).start()

    def total_copy(d):
        return remote(
            total.at[g], total.at[g], total_send.at[d], total_recv.at[g], member(up(g, d, GROUPS))
        )

    def total_arrived(j):
        return remote(total.at[j], total.at[j], total_send.at[0], total_recv.at[j], sibling)

    @pl.loop(1, GROUPS)
    def _(d):
        total_copy(d).start()

    acts_ready(far(1))
    acts_ready(far(2))
    chain(1, True)
    remote(cot_hbm, cot.at[tokens_of(other)], pair_send.at[0], pair_recv.at[0], sibling).wait_recv()

    @pl.loop(3, NZ)
    def _(i):
        acts_ready(far(i))

    def wave(i):
        return lax.rem(z + lax.div(i + 1, 2) * (2 * lax.rem(i, 2) - 1) + NZ, NZ)

    keys[...] = jnp.zeros_like(keys)

    def back_copy(zz, hi):
        return remote(
            back.at[zz, hi], grads.at[:, columns(hi, zz, c)], back_send.at[zz, hi], back_recv.at[zz, hi], sibling
        )

    def back_arrived(zz, hi):
        return remote(
            back.at[zz, hi], grads.at[:, columns(hi, zz, other)], back_send.at[zz, hi], back_recv.at[zz, hi], sibling
        )

    def back_of(rows, w):
        product = lax.dot_general(rows, w, (((1,), (1,)), ((), ())), preferred_element_type=F32)
        return (product * out_scale).astype(BF16)

    def multiply(zz):
        for hi in range(2):
            lower = [gathered[zz, :, 2 * hi + lo].reshape(block // 2, kw) for lo in range(2)]
            w = jnp.concatenate(lower, axis=0)
            back[zz, hi] = back_of(cot[tokens_of(other), :], w)
            back_copy(zz, hi).start()
            grads[:, columns(hi, zz, c)] = back_of(cot[tokens_of(c), :], w)
            keys[...] += jnp.dot(acts[zz, hi], w, preferred_element_type=F32)

    def cross_copy(h):
        return remote(
            cross_out.at[h], cross_in.at[h], cross_send.at[h], cross_recv.at[h], device(up(x, 2, NX), y, z, c)
        )

    def chain_end():
        for way in range(2):
            for k in (5, 6):
                chain_copy(way, k).wait_recv()
        for mine in range(2):
            hi = x_hi if mine else 1 - x_hi
            for h in range(2):
                done = share(h, z, hi) + chain_in[0, 6 - h, hi].astype(F32) + chain_in[1, 5 + h, hi].astype(F32)
                if mine:
                    cross_own[h] = done
                else:
                    cross_out[h] = done.astype(BF16)
                    cross_copy(h).start()

    def outer_results():
        for j in range(GROUPS):
            @pl.when(g != j)
            def _():
                total_arrived(j).wait_recv()

        for j in range(GROUPS):
            own = pl.ds(j * piece, piece)
            weights_out[own, :], moved_out[own, :] = nesterov(total[j], master[own, :], momentum[own, :])

    @pl.loop(1, NZ + LAG_END)
    def _(i):
        @pl.when(i < NZ)
        def _():
            zz = wave(i)
            z_arrived(zz).wait_recv()
            for d in range(1, NX):
                x_copy(zz, d).start()

        @pl.when(i < NZ + LAG_Y)
        def _():
            zz = wave(i - LAG_Y)
            for d in range(1, NX):
                x_arrived(zz, up(x, d, NX)).wait_recv()
            for way in range(2):
                y_copy(zz, way).start()

        @pl.when(jnp.logical_and(i >= LAG_F, i < NZ + LAG_F))
        def _():
            zz = wave(i - LAG_F)
            for way in range(2):
                y_arrived(zz, way).wait_recv()
            for way in range(2):
                f_copy(zz, way).start()

        @pl.when(i < 6)
        def _():
            chain(i + 1, False)

        @pl.when(i == 7)
        def _():
            chain_end()

        @pl.when(i == 3)
        def _():
            outer_results()

        @pl.when(i >= LAG_END)
        def _():
            zz = wave(i - LAG_END)
            for way in range(2):
                f_arrived(zz, way).wait_recv()
            multiply(zz)

    keys_copy = remote(keys.at[tokens_of(other)], keys_in, pair_send.at[1], pair_recv.at[1], sibling)
    keys_copy.start()

    for h in range(2):
        cross_copy(h).wait_recv()
        wgrad_out[pl.ds(h * half, half), :] = (cross_own[h] + cross_in[h].astype(F32)) * out_scale

    keys_copy.wait_recv()
    keys_out[...] = ((keys[tokens_of(c), :] + keys_in[...]) * out_scale).astype(BF16)

    cot_swap.wait_send()
    cot_t_swap.wait_send()
    keys_copy.wait_send()
    for h in range(2):
        cross_copy(h).wait_send()

    @pl.loop(0, NZ)
    def _(zz):
        for hi in range(2):
            act_swap(zz, hi).wait_send()
            back_copy(zz, hi).wait_send()
            back_arrived(zz, hi).wait_recv()
        for d in range(1, NX):
            x_copy(zz, d).wait_send()
        for way in range(2):
            y_copy(zz, way).wait_send()
            f_copy(zz, way).wait_send()

    @pl.loop(1, NZ)
    def _(d):
        coded_copy(d).wait_send()
        total_copy(d).wait_send()
        z_copy(d).wait_send()
        for way in range(2):
            chain_copy(way, d - 1).wait_send()


def finish(weights, moved, keys, grads, turned, weights_hbm, moved_hbm, keys_hbm, grads_hbm, wgrad_hbm, wgrad, sem):
    pairs = ((grads, grads_hbm), (weights, weights_hbm), (moved, moved_hbm), (keys, keys_hbm), (wgrad, wgrad_hbm))
    copies = [pltpu.make_async_copy(src, dst, sem.at[i]) for i, (src, dst) in enumerate(pairs)]
    for copy in copies[:4]:
        copy.start()
    wgrad[...] = turned[...].T
    copies[4].start()
    for copy in copies:
        copy.wait()


def body(delta_codes, master_weights, outer_momentum, activations, key_cotangent):
    tokens, width = activations.shape
    rows, kw = master_weights.shape
    block, piece, half = width // 32, width // 32 // GROUPS, kw // 2
    dma = pltpu.SemaphoreType.DMA
    hbm = pl.BlockSpec(memory_space=pl.ANY)
    vmem = pl.BlockSpec(memory_space=pltpu.VMEM)
    arguments = (delta_codes[0], master_weights, outer_momentum, activations, key_cotangent)
    results = pl.pallas_call(
        kernel,
        name="outer_step",
        out_shape=(
            pltpu.VMEM((rows, kw), F32),
            pltpu.VMEM((rows, kw), F32),
            pltpu.VMEM((tokens, kw), BF16),
            pltpu.VMEM((tokens, width), BF16),
            pltpu.VMEM((kw, block), F32),
        ),
        in_specs=[hbm] * 5,
        out_specs=(vmem,) * 5,
        scratch_shapes=[
            pltpu.VMEM((rows, kw), jnp.int32),
            pltpu.VMEM((rows, kw), F32),
            pltpu.VMEM((rows, kw), F32),
            pltpu.VMEM((2 * tokens, kw), BF16),
            pltpu.VMEM((2, 2, half, tokens), BF16),
            pltpu.VMEM((NZ, 2, 2 * tokens, block), BF16),
            pltpu.VMEM((GROUPS, piece, kw), BF16),
            pltpu.VMEM((GROUPS, piece, kw), BF16),
            pltpu.VMEM((GROUPS, piece, kw), BF16),
            pltpu.VMEM((NZ, NY, NX, piece, kw), BF16),
            pltpu.VMEM((2, 7, 2, half, block), BF16),
            pltpu.VMEM((2, 7, 2, half, block), BF16),
            pltpu.VMEM((2, half, block), BF16),
            pltpu.VMEM((2, half, block), BF16),
            pltpu.VMEM((2, half, block), F32),
            pltpu.VMEM((2 * tokens, kw), F32),
            pltpu.VMEM((tokens, kw), F32),
            pltpu.VMEM((NZ, 2, tokens, block), BF16),
            dma((4,)),
            dma((NZ, 2)),
            dma((NZ, 2)),
            dma((NZ, 2)),
            dma((3,)),
            dma((3,)),
            dma((GROUPS,)),
            dma((GROUPS,)),
            dma((GROUPS,)),
            dma((GROUPS,)),
            dma((NZ,)),
            dma((NZ,)),
            dma((NZ, NX)),
            dma((NZ, NX)),
            dma((NZ, 2)),
            dma((NZ, 2)),
            dma((NZ, 2)),
            dma((NZ, 2)),
            dma((2, 7)),
            dma((2, 7)),
            dma((2,)),
            dma((2,)),
            dma((NZ, 2)),
            dma((NZ, 2)),
        ],
        compiler_params=pltpu.CompilerParams(
            collective_id=0, has_side_effects=True, vmem_limit_bytes=44 * 2**20
        ),
        cost_estimate=pl.CostEstimate(
            flops=6 * tokens * width * kw, bytes_accessed=16 * 2**20, transcendentals=0
        ),
    )(*[pltpu.with_memory_space_constraint(a, pltpu.HBM) for a in arguments])
    weights, moved, keys, grads, wgrad = pl.pallas_call(
        finish,
        name="finish",
        out_shape=(
            jax.ShapeDtypeStruct((rows, kw), F32),
            jax.ShapeDtypeStruct((rows, kw), F32),
            jax.ShapeDtypeStruct((tokens, kw), BF16),
            jax.ShapeDtypeStruct((tokens, width), BF16),
            jax.ShapeDtypeStruct((rows, kw), F32),
        ),
        in_specs=[vmem] * 5,
        out_specs=(hbm,) * 5,
        scratch_shapes=[pltpu.VMEM((rows, kw), F32), dma((5,))],
        compiler_params=pltpu.CompilerParams(vmem_limit_bytes=16 * 2**20),
    )(*[pltpu.with_memory_space_constraint(r, pltpu.VMEM) for r in results])
    return weights, moved, keys, grads, wgrad[None]


def solution(mesh):
    placed = (
        P("group", "fsdp", None),
        P("fsdp", None),
        P("fsdp", None),
        P(("group", "fsdp"), None),
        P(("group", "fsdp"), None),
    )
    return jax.shard_map(
        body,
        mesh=mesh,
        in_specs=placed,
        out_specs=(
            P("fsdp", None),
            P("fsdp", None),
            P(("group", "fsdp"), None),
            P(("group", "fsdp"), None),
            P("group", "fsdp", None),
        ),
        check_vma=False,
    )
```

```python
import functools

import jax
import jax.numpy as jnp
from jax import lax
from jax.experimental import pallas as pl
from jax.experimental.pallas import tpu as pltpu
from jax.sharding import PartitionSpec as P

MESH = pl.DeviceIdType.MESH
F32 = jnp.float32
BF16 = jnp.bfloat16
NX, NY, NZ = 4, 4, 8
GROUPS = 8
LAG_Y, LAG_F, LAG_END = 1, 3, 5
CROSS_FIRST = 96


def device(x, y, z, c):
    return (lax.rem(x, 2) * 4 + y, lax.div(x, 2) * 16 + z * 2 + c)


def up(v, d, n):
    return lax.rem(v + d, n)


def dequantize(codes):
    values = codes.astype(F32)
    size = jnp.abs(values)
    largest = jnp.max(size, axis=-1, keepdims=True)
    scale = jnp.floor((largest + 0.5) / 127.0) + 1.0
    half = jnp.floor(scale * 0.5)
    magnitude = jnp.floor((size + half + 0.5) / scale)
    signed = jnp.where(values < 0.0, -magnitude, magnitude)
    return signed * scale * (1.0 / 4096.0)


def nesterov(total, weights, momentum):
    outer_grad = total.astype(F32) / GROUPS
    moved = 0.9 * momentum + outer_grad
    return weights - 0.7 * (outer_grad + 0.9 * moved), moved


def kernel(
    delta_hbm, master_hbm, momentum_hbm, acts_hbm, cot_hbm,
    weights_out, moved_out, keys_out, grads, wgrad_out,
    delta, master, momentum, cot, cot_t, late_t, early_t, acts,
    coded, coded_in, total, gathered,
    chain_out, chain_in, cross_out, cross_in, cross_own,
    first_out, first_in, line_out, line_in,
    keys, keys_in, back,
    load_sem, acts_load, acts_send, acts_recv, pair_send, pair_recv,
    coded_send, coded_recv, total_send, total_recv,
    z_send, z_recv, x_send, x_recv, y_send, y_recv, f_send, f_recv,
    chain_send, chain_recv, cross_send, cross_recv,
    first_send, first_recv, line_send, line_recv,
    back_send, back_recv,
):
    tokens, width = acts_hbm.shape
    kw = cot_hbm.shape[1]
    block = width // 32
    piece = block // GROUPS
    half = kw // 2
    late = half - CROSS_FIRST
    out_scale = width ** (-0.5)

    g, f = lax.axis_index("group"), lax.axis_index("fsdp")
    y, x_lo = lax.rem(g, NY), lax.div(g, NY)
    c, z, x_hi = lax.rem(f, 2), lax.rem(lax.div(f, 2), NZ), lax.div(f, 16)
    x = 2 * x_hi + x_lo
    other = 1 - c
    sibling = device(x, y, z, other)

    def member(j):
        return device(2 * x_hi + lax.div(j, NY), lax.rem(j, NY), z, c)

    def remote(src, dst, send, recv, to):
        return pltpu.make_async_remote_copy(
            src_ref=src, dst_ref=dst, send_sem=send, recv_sem=recv, device_id=to, device_id_type=MESH
        )

    def columns(hi, zz, core):
        return pl.ds(pl.multiple_of((hi * 16 + zz * 2 + core) * block, block), block)

    def tokens_of(core):
        return pl.ds(pl.multiple_of(core * tokens, tokens), tokens)

    loads = [
        pltpu.make_async_copy(delta_hbm, delta, load_sem.at[0]),
        pltpu.make_async_copy(cot_hbm, cot.at[tokens_of(c)], load_sem.at[1]),
        pltpu.make_async_copy(master_hbm, master, load_sem.at[2]),
        pltpu.make_async_copy(momentum_hbm, momentum, load_sem.at[3]),
    ]
    for load in loads:
        load.start()

    def act_load(zz, hi):
        return pltpu.make_async_copy(
            acts_hbm.at[:, columns(hi, zz, c)], acts.at[zz, hi, tokens_of(c)], acts_load.at[zz, hi]
        )

    def act_swap(zz, hi):
        return remote(
            acts_hbm.at[:, columns(hi, zz, other)], acts.at[zz, hi, tokens_of(c)],
            acts_send.at[zz, hi], acts_recv.at[zz, hi], sibling,
        )

    def act_arrived(zz, hi):
        return remote(
            acts_hbm.at[:, columns(hi, zz, other)], acts.at[zz, hi, tokens_of(other)],
            acts_send.at[zz, hi], acts_recv.at[zz, hi], sibling,
        )

    def far(i):
        step = lax.div(i + 1, 2)
        return lax.rem(z + 4 + step * (2 * lax.rem(i, 2) - 1) * -1 + NZ, NZ)

    @pl.loop(0, NZ)
    def _(i):
        for hi in range(2):
            act_load(far(i), hi).start()

    partners = [sibling]
    partners += [device(x, y, up(z, d, NZ), c) for d in (1, NZ - 1)]
    partners += [device(up(x, d, NX), y, z, c) for d in range(1, NX)]
    partners += [device(x, up(y, d, NY), z, c) for d in range(1, NY)]
    partners += [device(2 * x_hi + 1 - x_lo, up(y, d, NY), z, c) for d in range(1, NY)]
    barrier = pltpu.get_barrier_semaphore()
    for partner in partners:
        pl.semaphore_signal(barrier, inc=1, device_id=partner, device_id_type=MESH)

    loads[0].wait()
    for j in range(GROUPS):
        for k in range(kw // 128):
            codes = delta[pl.ds(j * piece, piece), pl.ds(k * 128, 128)]
            coded[j, :, pl.ds(k * 128, 128)] = dequantize(codes).astype(BF16)
    loads[1].wait()
    cot_t[c] = cot[tokens_of(c), :].T.reshape(2, half, tokens)
    pl.semaphore_wait(barrier, len(partners))

    def coded_copy(d):
        j = up(g, d, GROUPS)
        return remote(coded.at[j], coded_in.at[g], coded_send.at[d], coded_recv.at[g], member(j))

    def coded_arrived(j):
        return remote(coded.at[j], coded_in.at[j], coded_send.at[0], coded_recv.at[j], sibling)

    @pl.loop(1, GROUPS)
    def _(d):
        coded_copy(d).start()

    cot_swap = remote(cot_hbm, cot.at[tokens_of(c)], pair_send.at[0], pair_recv.at[0], sibling)
    cot_swap.start()
    cot_t_swap = remote(cot_t.at[c], cot_t.at[c], pair_send.at[2], pair_recv.at[2], sibling)
    cot_t_swap.start()

    @pl.loop(0, NZ)
    def _(i):
        for hi in range(2):
            act_swap(far(i), hi).start()


    def acts_ready(zz):
        for hi in range(2):
            act_load(zz, hi).wait()
            act_arrived(zz, hi).wait_recv()

    def chain_copy(way, k):
        to = device(x, y, up(z, 1 if way == 0 else NZ - 1, NZ), c)
        return remote(
            chain_out.at[way, k], chain_in.at[way, k], chain_send.at[way, k], chain_recv.at[way, k], to
        )

    def share(h, zz, hi):
        return jnp.dot(late_t[h], acts[zz, hi], preferred_element_type=F32)

    def early_share(h, zz, hi):
        return jnp.dot(early_t[h], acts[zz, hi], preferred_element_type=F32)

    def first_copy(zz):
        return remote(
            first_out.at[zz], first_in.at[zz], first_send.at[zz], first_recv.at[zz], device(up(x, 2, NX), y, z, c)
        )

    def first(i):
        zz = far(i)
        for h in range(2):
            first_out[zz, h] = early_share(h, zz, 1 - x_hi).astype(BF16)
        first_copy(zz).start()

    def line_copy(way, k):
        to = device(x, y, up(z, 1 if way == 0 else NZ - 1, NZ), c)
        return remote(line_out.at[way, k], line_in.at[way, k], line_send.at[way, k], line_recv.at[way, k], to)

    def line(k, opening):
        s = lax.div(k + 1, 2)
        for way in range(2):
            zz = up(z, 4 - s if way == 0 else 4 + s, NZ)
            h = lax.rem(k + way, 2)
            if not opening:
                line_copy(way, k - 2).wait_recv()
            sent = early_share(h, zz, x_hi) + first_in[zz, h].astype(F32)
            if not opening:
                sent += line_in[way, k - 2].astype(F32)
            line_out[way, k] = sent.astype(BF16)
            line_copy(way, k).start()

    def line_end():
        first_copy(z).wait_recv()
        for way in range(2):
            for k in (5, 6):
                line_copy(way, k).wait_recv()
        for h in range(2):
            done = early_share(h, z, x_hi) + first_in[z, h].astype(F32)
            done += line_in[0, 6 - h].astype(F32) + line_in[1, 5 + h].astype(F32)
            wgrad_out[pl.ds(h * half + late, CROSS_FIRST), :] = done * out_scale

    def chain(k, first):
        s = lax.div(k + 1, 2)
        for way in range(2):
            zz = up(z, 4 - s if way == 0 else 4 + s, NZ)
            h = lax.rem(k + way, 2)
            if not first:
                chain_copy(way, k - 2).wait_recv()
            for hi in range(2):
                sent = share(h, zz, hi)
                if not first:
                    sent += chain_in[way, k - 2, hi].astype(F32)
                chain_out[way, k, hi] = sent.astype(BF16)
            chain_copy(way, k).start()

    remote(cot_t.at[other], cot_t.at[other], pair_send.at[2], pair_recv.at[2], sibling).wait_recv()
    for h in range(2):
        for core in range(2):
            late_t[h, :, pl.ds(core * tokens, tokens)] = cot_t[core, h, :late]
            early_t[h, :, pl.ds(core * tokens, tokens)] = cot_t[core, h, late:]
    acts_ready(far(0))
    chain(0, True)
    first(0)

    rows = pl.ds(pl.multiple_of(g * piece, piece), piece)

    @pl.loop(1, GROUPS)
    def _(d):
        coded_arrived(up(g, d, GROUPS)).wait_recv()

    summed = coded[g].astype(F32)
    for d in range(1, GROUPS):
        summed += coded_in[up(g, d, GROUPS)].astype(F32)
    total[g] = summed.astype(BF16)
    loads[2].wait()
    loads[3].wait()
    updated, _ = nesterov(total[g], master[rows, :], momentum[rows, :])
    gathered[z, y, x] = updated.astype(BF16)

    def z_copy(zz, way):
        to = device(x, y, up(z, 1 if way == 0 else NZ - 1, NZ), c)
        return remote(gathered.at[zz, y, x], gathered.at[zz, y, x], z_send.at[zz, way], z_recv.at[zz], to)

    def z_arrived(zz):
        return remote(gathered.at[zz, y, x], gathered.at[zz, y, x], z_send.at[zz, 0], z_recv.at[zz], sibling)

    def x_copy(zz, d):
        return remote(
            gathered.at[zz, y, x], gathered.at[zz, y, x], x_send.at[zz, d], x_recv.at[zz, x],
            device(up(x, d, NX), y, z, c),
        )

    def x_arrived(zz, xx):
        return remote(
            gathered.at[zz, y, xx], gathered.at[zz, y, xx], x_send.at[zz, 0], x_recv.at[zz, xx], sibling
        )

    def y_copy(zz, way):
        to = device(x, up(y, 1 if way == 0 else NY - 1, NY), z, c)
        return remote(gathered.at[zz, y], gathered.at[zz, y], y_send.at[zz, way], y_recv.at[zz, way], to)

    def y_arrived(zz, way):
        yy = up(y, NY - 1 if way == 0 else 1, NY)
        return remote(
            gathered.at[zz, yy], gathered.at[zz, yy], y_send.at[zz, way], y_recv.at[zz, way], sibling
        )

    def f_copy(zz, way):
        yy = up(y, NY - 1 if way == 0 else 1, NY)
        to = device(x, up(y, 1 if way == 0 else NY - 1, NY), z, c)
        part = gathered.at[zz, yy, pl.ds(way * 2, 2)]
        return remote(part, part, f_send.at[zz, way], f_recv.at[zz, way], to)

    def f_arrived(zz, way):
        part = gathered.at[zz, up(y, 2, NY), pl.ds(way * 2, 2)]
        return remote(part, part, f_send.at[zz, way], f_recv.at[zz, way], sibling)

    for way in range(2):
        z_copy(z, way).start()
    for d in range(1, NX):
        x_copy(z, d).start()

    def total_copy(d):
        return remote(
            total.at[g], total.at[g], total_send.at[d], total_recv.at[g], member(up(g, d, GROUPS))
        )

    def total_arrived(j):
        return remote(total.at[j], total.at[j], total_send.at[0], total_recv.at[j], sibling)

    @pl.loop(1, GROUPS)
    def _(d):
        total_copy(d).start()

    acts_ready(far(1))
    acts_ready(far(2))
    chain(1, True)
    first(1)
    first(2)
    remote(cot_hbm, cot.at[tokens_of(other)], pair_send.at[0], pair_recv.at[0], sibling).wait_recv()

    @pl.loop(3, NZ)
    def _(i):
        acts_ready(far(i))

    def wave(i):
        return lax.rem(z + lax.div(i + 1, 2) * (2 * lax.rem(i, 2) - 1) + NZ, NZ)

    keys[...] = jnp.zeros_like(keys)

    def back_copy(zz, hi):
        return remote(
            back.at[zz, hi], grads.at[:, columns(hi, zz, c)], back_send.at[zz, hi], back_recv.at[zz, hi], sibling
        )

    def back_arrived(zz, hi):
        return remote(
            back.at[zz, hi], grads.at[:, columns(hi, zz, other)], back_send.at[zz, hi], back_recv.at[zz, hi], sibling
        )

    def back_of(rows, w):
        product = lax.dot_general(rows, w, (((1,), (1,)), ((), ())), preferred_element_type=F32)
        return (product * out_scale).astype(BF16)

    def multiply(zz):
        for hi in range(2):
            lower = [gathered[zz, :, 2 * hi + lo].reshape(block // 2, kw) for lo in range(2)]
            w = jnp.concatenate(lower, axis=0)
            back[zz, hi] = back_of(cot[tokens_of(other), :], w)
            back_copy(zz, hi).start()
            grads[:, columns(hi, zz, c)] = back_of(cot[tokens_of(c), :], w)
            keys[...] += jnp.dot(acts[zz, hi], w, preferred_element_type=F32)

    def cross_copy(h):
        return remote(
            cross_out.at[h], cross_in.at[h], cross_send.at[h], cross_recv.at[h], device(up(x, 2, NX), y, z, c)
        )

    def chain_end():
        for way in range(2):
            for k in (5, 6):
                chain_copy(way, k).wait_recv()
        for mine in range(2):
            hi = x_hi if mine else 1 - x_hi
            for h in range(2):
                done = share(h, z, hi) + chain_in[0, 6 - h, hi].astype(F32) + chain_in[1, 5 + h, hi].astype(F32)
                if mine:
                    cross_own[h] = done
                else:
                    cross_out[h] = done.astype(BF16)
                    cross_copy(h).start()

    def outer_results():
        for j in range(GROUPS):
            @pl.when(g != j)
            def _():
                total_arrived(j).wait_recv()

        for j in range(GROUPS):
            own = pl.ds(j * piece, piece)
            weights_out[own, :], moved_out[own, :] = nesterov(total[j], master[own, :], momentum[own, :])

    @pl.loop(1, NZ + LAG_END)
    def _(i):
        @pl.when(i < NZ)
        def _():
            zz = wave(i)
            z_arrived(zz).wait_recv()

            @pl.when(jnp.logical_and(lax.rem(i, 2) == 1, i < 7))
            def _():
                z_copy(zz, 1).start()

            @pl.when(jnp.logical_and(lax.rem(i, 2) == 0, i < 6))
            def _():
                z_copy(zz, 0).start()

            for d in range(1, NX):
                x_copy(zz, d).start()

        @pl.when(i < NZ + LAG_Y)
        def _():
            zz = wave(i - LAG_Y)
            for d in range(1, NX):
                x_arrived(zz, up(x, d, NX)).wait_recv()
            for way in range(2):
                y_copy(zz, way).start()

        @pl.when(jnp.logical_and(i >= LAG_F, i < NZ + LAG_F))
        def _():
            zz = wave(i - LAG_F)
            for way in range(2):
                y_arrived(zz, way).wait_recv()
            for way in range(2):
                f_copy(zz, way).start()

        @pl.when(i < 6)
        def _():
            chain(i + 1, False)
            first(i + 2)

        @pl.when(i == 1)
        def _():
            first_copy(far(0)).wait_recv()
            line(0, True)

        @pl.when(i == 2)
        def _():
            first_copy(far(1)).wait_recv()
            first_copy(far(2)).wait_recv()
            line(1, True)

        @pl.when(jnp.logical_or(i == 4, i == 6))
        def _():
            first_copy(far(i - 1)).wait_recv()
            first_copy(far(i)).wait_recv()

        @pl.when(jnp.logical_and(i >= 3, i < 8))
        def _():
            line(i - 1, False)

        @pl.when(i == 7)
        def _():
            chain_end()

        @pl.when(i == 9)
        def _():
            line_end()

        @pl.when(i == 3)
        def _():
            outer_results()

        @pl.when(i >= LAG_END)
        def _():
            zz = wave(i - LAG_END)
            for way in range(2):
                f_arrived(zz, way).wait_recv()
            multiply(zz)

    keys_copy = remote(keys.at[tokens_of(other)], keys_in, pair_send.at[1], pair_recv.at[1], sibling)
    keys_copy.start()

    for h in range(2):
        cross_copy(h).wait_recv()
        wgrad_out[pl.ds(h * half, late), :] = (cross_own[h] + cross_in[h].astype(F32)) * out_scale

    keys_copy.wait_recv()
    keys_out[...] = ((keys[tokens_of(c), :] + keys_in[...]) * out_scale).astype(BF16)

    cot_swap.wait_send()
    cot_t_swap.wait_send()
    keys_copy.wait_send()
    for h in range(2):
        cross_copy(h).wait_send()

    @pl.loop(0, NZ)
    def _(zz):
        for hi in range(2):
            act_swap(zz, hi).wait_send()
            back_copy(zz, hi).wait_send()
            back_arrived(zz, hi).wait_recv()
        first_copy(zz).wait_send()
        for d in range(1, NX):
            x_copy(zz, d).wait_send()
        for way in range(2):
            y_copy(zz, way).wait_send()
            f_copy(zz, way).wait_send()

    @pl.loop(0, 4)
    def _(d):
        z_copy(up(z, d, NZ), 1).wait_send()

    @pl.loop(0, 3)
    def _(d):
        z_copy(up(z, NZ - d, NZ), 0).wait_send()

    @pl.loop(1, NZ)
    def _(d):
        coded_copy(d).wait_send()
        total_copy(d).wait_send()
        for way in range(2):
            chain_copy(way, d - 1).wait_send()
            line_copy(way, d - 1).wait_send()


def finish(weights, moved, keys, grads, turned, weights_hbm, moved_hbm, keys_hbm, grads_hbm, wgrad_hbm, wgrad, sem):
    pairs = ((grads, grads_hbm), (weights, weights_hbm), (moved, moved_hbm), (keys, keys_hbm), (wgrad, wgrad_hbm))
    copies = [pltpu.make_async_copy(src, dst, sem.at[i]) for i, (src, dst) in enumerate(pairs)]
    for copy in copies[:4]:
        copy.start()
    wgrad[...] = turned[...].T
    copies[4].start()
    for copy in copies:
        copy.wait()


def body(delta_codes, master_weights, outer_momentum, activations, key_cotangent):
    tokens, width = activations.shape
    rows, kw = master_weights.shape
    block, piece, half = width // 32, width // 32 // GROUPS, kw // 2
    late = half - CROSS_FIRST
    dma = pltpu.SemaphoreType.DMA
    hbm = pl.BlockSpec(memory_space=pl.ANY)
    vmem = pl.BlockSpec(memory_space=pltpu.VMEM)
    arguments = (delta_codes[0], master_weights, outer_momentum, activations, key_cotangent)
    results = pl.pallas_call(
        kernel,
        name="outer_step",
        out_shape=(
            pltpu.VMEM((rows, kw), F32),
            pltpu.VMEM((rows, kw), F32),
            pltpu.VMEM((tokens, kw), BF16),
            pltpu.VMEM((tokens, width), BF16),
            pltpu.VMEM((kw, block), F32),
        ),
        in_specs=[hbm] * 5,
        out_specs=(vmem,) * 5,
        scratch_shapes=[
            pltpu.VMEM((rows, kw), jnp.int32),
            pltpu.VMEM((rows, kw), F32),
            pltpu.VMEM((rows, kw), F32),
            pltpu.VMEM((2 * tokens, kw), BF16),
            pltpu.VMEM((2, 2, half, tokens), BF16),
            pltpu.VMEM((2, late, 2 * tokens), BF16),
            pltpu.VMEM((2, CROSS_FIRST, 2 * tokens), BF16),
            pltpu.VMEM((NZ, 2, 2 * tokens, block), BF16),
            pltpu.VMEM((GROUPS, piece, kw), BF16),
            pltpu.VMEM((GROUPS, piece, kw), BF16),
            pltpu.VMEM((GROUPS, piece, kw), BF16),
            pltpu.VMEM((NZ, NY, NX, piece, kw), BF16),
            pltpu.VMEM((2, 7, 2, late, block), BF16),
            pltpu.VMEM((2, 7, 2, late, block), BF16),
            pltpu.VMEM((2, late, block), BF16),
            pltpu.VMEM((2, late, block), BF16),
            pltpu.VMEM((2, late, block), F32),
            pltpu.VMEM((NZ, 2, CROSS_FIRST, block), BF16),
            pltpu.VMEM((NZ, 2, CROSS_FIRST, block), BF16),
            pltpu.VMEM((2, 7, CROSS_FIRST, block), BF16),
            pltpu.VMEM((2, 7, CROSS_FIRST, block), BF16),
            pltpu.VMEM((2 * tokens, kw), F32),
            pltpu.VMEM((tokens, kw), F32),
            pltpu.VMEM((NZ, 2, tokens, block), BF16),
            dma((4,)),
            dma((NZ, 2)),
            dma((NZ, 2)),
            dma((NZ, 2)),
            dma((3,)),
            dma((3,)),
            dma((GROUPS,)),
            dma((GROUPS,)),
            dma((GROUPS,)),
            dma((GROUPS,)),
            dma((NZ, 2)),
            dma((NZ,)),
            dma((NZ, NX)),
            dma((NZ, NX)),
            dma((NZ, 2)),
            dma((NZ, 2)),
            dma((NZ, 2)),
            dma((NZ, 2)),
            dma((2, 7)),
            dma((2, 7)),
            dma((2,)),
            dma((2,)),
            dma((NZ,)),
            dma((NZ,)),
            dma((2, 7)),
            dma((2, 7)),
            dma((NZ, 2)),
            dma((NZ, 2)),
        ],
        compiler_params=pltpu.CompilerParams(
            collective_id=0, has_side_effects=True, vmem_limit_bytes=44 * 2**20
        ),
        cost_estimate=pl.CostEstimate(
            flops=6 * tokens * width * kw, bytes_accessed=16 * 2**20, transcendentals=0
        ),
    )(*[pltpu.with_memory_space_constraint(a, pltpu.HBM) for a in arguments])
    weights, moved, keys, grads, wgrad = pl.pallas_call(
        finish,
        name="finish",
        out_shape=(
            jax.ShapeDtypeStruct((rows, kw), F32),
            jax.ShapeDtypeStruct((rows, kw), F32),
            jax.ShapeDtypeStruct((tokens, kw), BF16),
            jax.ShapeDtypeStruct((tokens, width), BF16),
            jax.ShapeDtypeStruct((rows, kw), F32),
        ),
        in_specs=[vmem] * 5,
        out_specs=(hbm,) * 5,
        scratch_shapes=[pltpu.VMEM((rows, kw), F32), dma((5,))],
        compiler_params=pltpu.CompilerParams(vmem_limit_bytes=16 * 2**20),
    )(*[pltpu.with_memory_space_constraint(r, pltpu.VMEM) for r in results])
    return weights, moved, keys, grads, wgrad[None]


def solution(mesh):
    placed = (
        P("group", "fsdp", None),
        P("fsdp", None),
        P("fsdp", None),
        P(("group", "fsdp"), None),
        P(("group", "fsdp"), None),
    )
    return jax.shard_map(
        body,
        mesh=mesh,
        in_specs=placed,
        out_specs=(
            P("fsdp", None),
            P("fsdp", None),
            P(("group", "fsdp"), None),
            P(("group", "fsdp"), None),
            P("group", "fsdp", None),
        ),
        check_vma=False,
    )
```

```python
import functools

import jax
import jax.numpy as jnp
from jax import lax
from jax.experimental import pallas as pl
from jax.experimental.pallas import tpu as pltpu
from jax.sharding import PartitionSpec as P

MESH = pl.DeviceIdType.MESH
F32 = jnp.float32
BF16 = jnp.bfloat16
NX, NY, NZ = 4, 4, 8
GROUPS = 8
LAG_Y, LAG_F, LAG_END = 1, 3, 5
LINE_EARLY = 0
TOTAL_AT = 2
ORDER = ("near", "line", "total", "row", "far", "first", "last", "chain")
CROSS_FIRST = 80
TURNED = (4, 6)


def device(x, y, z, c):
    return (lax.rem(x, 2) * 4 + y, lax.div(x, 2) * 16 + z * 2 + c)


def up(v, d, n):
    return lax.rem(v + d, n)


def dequantize(codes):
    values = codes.astype(F32)
    size = jnp.abs(values)
    largest = jnp.max(size, axis=-1, keepdims=True)
    scale = jnp.floor((largest + 0.5) / 127.0) + 1.0
    half = jnp.floor(scale * 0.5)
    magnitude = jnp.floor((size + half + 0.5) / scale)
    signed = jnp.where(values < 0.0, -magnitude, magnitude)
    return signed * scale * (1.0 / 4096.0)


def nesterov(total, weights, momentum):
    outer_grad = total.astype(F32) / GROUPS
    moved = 0.9 * momentum + outer_grad
    return weights - 0.7 * (outer_grad + 0.9 * moved), moved


def kernel(
    delta_hbm, master_hbm, momentum_hbm, acts_hbm, cot_hbm,
    weights_out, moved_out, keys_out, grads, wgrad_out,
    delta, master, momentum, cot, cot_t, late_t, early_t, acts,
    coded, coded_in, total, gathered,
    chain_out, chain_in, cross_out, cross_in, cross_own,
    first_out, first_in, line_out, line_in,
    keys, keys_in, back,
    load_sem, acts_load, acts_send, acts_recv, pair_send, pair_recv,
    coded_send, coded_recv, total_send, total_recv,
    z_send, z_recv, x_send, x_recv, y_send, y_recv, f_send, f_recv,
    chain_send, chain_recv, cross_send, cross_recv,
    first_send, first_recv, line_send, line_recv,
    back_send, back_recv,
):
    tokens, width = acts_hbm.shape
    kw = cot_hbm.shape[1]
    block = width // 32
    piece = block // GROUPS
    half = kw // 2
    late = half - CROSS_FIRST
    out_scale = width ** (-0.5)

    g, f = lax.axis_index("group"), lax.axis_index("fsdp")
    y, x_lo = lax.rem(g, NY), lax.div(g, NY)
    c, z, x_hi = lax.rem(f, 2), lax.rem(lax.div(f, 2), NZ), lax.div(f, 16)
    x = 2 * x_hi + x_lo
    other = 1 - c
    sibling = device(x, y, z, other)

    def member(j):
        return device(2 * x_hi + lax.div(j, NY), lax.rem(j, NY), z, c)

    def remote(src, dst, send, recv, to):
        return pltpu.make_async_remote_copy(
            src_ref=src, dst_ref=dst, send_sem=send, recv_sem=recv, device_id=to, device_id_type=MESH
        )

    def columns(hi, zz, core):
        return pl.ds(pl.multiple_of((hi * 16 + zz * 2 + core) * block, block), block)

    def tokens_of(core):
        return pl.ds(pl.multiple_of(core * tokens, tokens), tokens)

    loads = [
        pltpu.make_async_copy(delta_hbm, delta, load_sem.at[0]),
        pltpu.make_async_copy(cot_hbm, cot.at[tokens_of(c)], load_sem.at[1]),
        pltpu.make_async_copy(master_hbm, master, load_sem.at[2]),
        pltpu.make_async_copy(momentum_hbm, momentum, load_sem.at[3]),
    ]
    for load in loads:
        load.start()

    def act_load(zz, hi):
        return pltpu.make_async_copy(
            acts_hbm.at[:, columns(hi, zz, c)], acts.at[zz, hi, tokens_of(c)], acts_load.at[zz, hi]
        )

    def act_swap(zz, hi):
        return remote(
            acts_hbm.at[:, columns(hi, zz, other)], acts.at[zz, hi, tokens_of(c)],
            acts_send.at[zz, hi], acts_recv.at[zz, hi], sibling,
        )

    def act_arrived(zz, hi):
        return remote(
            acts_hbm.at[:, columns(hi, zz, other)], acts.at[zz, hi, tokens_of(other)],
            acts_send.at[zz, hi], acts_recv.at[zz, hi], sibling,
        )

    def far(i):
        step = lax.div(i + 1, 2)
        return lax.rem(z + 4 + step * (2 * lax.rem(i, 2) - 1) * -1 + NZ, NZ)

    @pl.loop(0, NZ)
    def _(i):
        for hi in range(2):
            act_load(far(i), hi).start()

    partners = [sibling]
    partners += [device(x, y, up(z, d, NZ), c) for d in (1, NZ - 1)]
    partners += [device(up(x, d, NX), y, z, c) for d in range(1, NX)]
    partners += [device(x, up(y, d, NY), z, c) for d in range(1, NY)]
    partners += [device(2 * x_hi + 1 - x_lo, up(y, d, NY), z, c) for d in range(1, NY)]
    barrier = pltpu.get_barrier_semaphore()
    for partner in partners:
        pl.semaphore_signal(barrier, inc=1, device_id=partner, device_id_type=MESH)

    loads[0].wait()
    for j in range(GROUPS):
        for k in range(kw // 128):
            codes = delta[pl.ds(j * piece, piece), pl.ds(k * 128, 128)]
            coded[j, :, pl.ds(k * 128, 128)] = dequantize(codes).astype(BF16)
    loads[1].wait()
    cot_t[c] = cot[tokens_of(c), :].T.reshape(2, half, tokens)
    pl.semaphore_wait(barrier, len(partners))

    def coded_copy(d):
        j = up(g, d, GROUPS)
        return remote(coded.at[j], coded_in.at[g], coded_send.at[d], coded_recv.at[g], member(j))

    def coded_arrived(j):
        return remote(coded.at[j], coded_in.at[j], coded_send.at[0], coded_recv.at[j], sibling)

    @pl.loop(1, GROUPS)
    def _(d):
        coded_copy(d).start()

    cot_swap = remote(cot_hbm, cot.at[tokens_of(c)], pair_send.at[0], pair_recv.at[0], sibling)
    cot_swap.start()
    cot_t_swap = remote(cot_t.at[c], cot_t.at[c], pair_send.at[2], pair_recv.at[2], sibling)
    cot_t_swap.start()

    @pl.loop(0, NZ)
    def _(i):
        for hi in range(2):
            act_swap(far(i), hi).start()


    def acts_ready(zz):
        for hi in range(2):
            act_load(zz, hi).wait()
            act_arrived(zz, hi).wait_recv()

    def chain_copy(way, k, part):
        to = device(x, y, up(z, 1 if way == 0 else NZ - 1, NZ), c)
        return remote(
            chain_out.at[way, k, part], chain_in.at[way, k, part],
            chain_send.at[way, k, part], chain_recv.at[way, k, part], to,
        )

    def share(h, zz, hi):
        return jnp.dot(late_t[h], acts[zz, hi], preferred_element_type=F32)

    def early_share(h, zz, hi):
        return jnp.dot(early_t[h], acts[zz, hi], preferred_element_type=F32)

    def first_copy(zz):
        return remote(
            first_out.at[zz], first_in.at[zz], first_send.at[zz], first_recv.at[zz], device(up(x, 2, NX), y, z, c)
        )

    def first(i):
        zz = far(i)
        for h in range(2):
            first_out[zz, h] = early_share(h, zz, 1 - x_hi).astype(BF16)
        first_copy(zz).start()

    def line_copy(way, k):
        to = device(x, y, up(z, 1 if way == 0 else NZ - 1, NZ), c)
        return remote(line_out.at[way, k], line_in.at[way, k], line_send.at[way, k], line_recv.at[way, k], to)

    def line(k, opening):
        s = lax.div(k + 1, 2)
        for way in range(2):
            zz = up(z, 4 - s if way == 0 else 4 + s, NZ)
            h = lax.rem(k + way, 2)
            if not opening:
                line_copy(way, k - 2).wait_recv()
            sent = early_share(h, zz, x_hi) + first_in[zz, h].astype(F32)
            if not opening:
                sent += line_in[way, k - 2].astype(F32)
            line_out[way, k] = sent.astype(BF16)
            line_copy(way, k).start()

    def line_end():
        first_copy(z).wait_recv()
        for way in range(2):
            for k in (5, 6):
                line_copy(way, k).wait_recv()
        for h in range(2):
            done = early_share(h, z, x_hi) + first_in[z, h].astype(F32)
            done += line_in[0, 6 - h].astype(F32) + line_in[1, 5 + h].astype(F32)
            wgrad_out[pl.ds(h * half + late, CROSS_FIRST), :] = done * out_scale

    def chain(k, opening):
        s = lax.div(k + 1, 2)
        for part in range(2):
            for way in range(2):
                zz = up(z, 4 - s if way == 0 else 4 + s, NZ)
                h = lax.rem(k + way, 2)
                sent = share(h, zz, x_hi if part else 1 - x_hi)
                if not opening:
                    chain_copy(way, k - 2, part).wait_recv()
                    sent += chain_in[way, k - 2, part].astype(F32)
                chain_out[way, k, part] = sent.astype(BF16)
                chain_copy(way, k, part).start()

    remote(cot_t.at[other], cot_t.at[other], pair_send.at[2], pair_recv.at[2], sibling).wait_recv()
    for h in range(2):
        for core in range(2):
            late_t[h, :, pl.ds(core * tokens, tokens)] = cot_t[core, h, :late]
            early_t[h, :, pl.ds(core * tokens, tokens)] = cot_t[core, h, late:]
    acts_ready(far(0))
    chain(0, True)
    first(0)

    rows = pl.ds(pl.multiple_of(g * piece, piece), piece)

    @pl.loop(1, GROUPS)
    def _(d):
        coded_arrived(up(g, d, GROUPS)).wait_recv()

    summed = coded[g].astype(F32)
    for d in range(1, GROUPS):
        summed += coded_in[up(g, d, GROUPS)].astype(F32)
    total[g] = summed.astype(BF16)
    loads[2].wait()
    loads[3].wait()
    updated, _ = nesterov(total[g], master[rows, :], momentum[rows, :])
    gathered[z, y, x] = updated.astype(BF16)

    def z_copy(zz, way):
        to = device(x, y, up(z, 1 if way == 0 else NZ - 1, NZ), c)
        return remote(gathered.at[zz, y, x], gathered.at[zz, y, x], z_send.at[zz, way], z_recv.at[zz], to)

    def z_arrived(zz):
        return remote(gathered.at[zz, y, x], gathered.at[zz, y, x], z_send.at[zz, 0], z_recv.at[zz], sibling)

    def near_copy(zz, d, turned):
        to = device(x, up(y, d, NY), z, c) if turned else device(up(x, d, NX), y, z, c)
        part = gathered.at[zz, y, x]
        return remote(part, part, x_send.at[zz, d], x_recv.at[zz, y if turned else x], to)

    def near_arrived(zz, d, turned):
        at = up(y if turned else x, d, NX)
        part = gathered.at[zz, at, x] if turned else gathered.at[zz, y, at]
        return remote(part, part, x_send.at[zz, 0], x_recv.at[zz, at], sibling)

    def neighbour(way, turned):
        d = 1 if way == 0 else NX - 1
        return device(up(x, d, NX), y, z, c) if turned else device(x, up(y, d, NY), z, c)

    def line_of(zz, d, turned):
        return gathered.at[zz, :, up(x, d, NX)] if turned else gathered.at[zz, up(y, d, NY)]

    def half_of(zz, d, way, turned):
        if turned:
            return gathered.at[zz, pl.ds(way * 2, 2), up(x, d, NX)]
        return gathered.at[zz, up(y, d, NY), pl.ds(way * 2, 2)]

    def y_copy(zz, way, turned):
        part = line_of(zz, 0, turned)
        return remote(part, part, y_send.at[zz, way], y_recv.at[zz, way], neighbour(way, turned))

    def y_arrived(zz, way, turned):
        part = line_of(zz, 3 if way == 0 else 1, turned)
        return remote(part, part, y_send.at[zz, way], y_recv.at[zz, way], sibling)

    def f_copy(zz, way, turned):
        part = half_of(zz, 3 if way == 0 else 1, way, turned)
        return remote(part, part, f_send.at[zz, way], f_recv.at[zz, way], neighbour(way, turned))

    def f_arrived(zz, way, turned):
        part = half_of(zz, 2, way, turned)
        return remote(part, part, f_send.at[zz, way], f_recv.at[zz, way], sibling)

    def either(i, step):
        if isinstance(i, int):
            step(i in TURNED)
            return
        hit = i == -1
        for t in TURNED:
            hit = jnp.logical_or(hit, i == t)
        pl.when(hit)(lambda: step(True))
        pl.when(jnp.logical_not(hit))(lambda: step(False))

    def stage_near(i, zz):
        def step(turned):
            for d in range(1, NX):
                near_copy(zz, d, turned).start()

        either(i, step)

    def stage_line(i, zz):
        def step(turned):
            for d in range(1, NX):
                near_arrived(zz, d, turned).wait_recv()
            for way in range(2):
                y_copy(zz, way, turned).start()

        either(i, step)

    def stage_far(i, zz):
        def step(turned):
            for way in range(2):
                y_arrived(zz, way, turned).wait_recv()
            for way in range(2):
                f_copy(zz, way, turned).start()

        either(i, step)

    def stage_last(i, zz):
        def step(turned):
            for way in range(2):
                f_arrived(zz, way, turned).wait_recv()

        either(i, step)

    def stage_sent(i, zz):
        def step(turned):
            for d in range(1, NX):
                near_copy(zz, d, turned).wait_send()
            for way in range(2):
                y_copy(zz, way, turned).wait_send()
                f_copy(zz, way, turned).wait_send()

        either(i, step)

    for way in range(2):
        z_copy(z, way).start()
    stage_near(0, z)

    def total_copy(d):
        return remote(
            total.at[g], total.at[g], total_send.at[d], total_recv.at[g], member(up(g, d, GROUPS))
        )

    def total_arrived(j):
        return remote(total.at[j], total.at[j], total_send.at[0], total_recv.at[j], sibling)

    acts_ready(far(1))
    acts_ready(far(2))
    chain(1, True)
    first(1)
    first(2)
    remote(cot_hbm, cot.at[tokens_of(other)], pair_send.at[0], pair_recv.at[0], sibling).wait_recv()

    @pl.loop(3, NZ)
    def _(i):
        acts_ready(far(i))

    def wave(i):
        return lax.rem(z + lax.div(i + 1, 2) * (2 * lax.rem(i, 2) - 1) + NZ, NZ)

    keys[...] = jnp.zeros_like(keys)

    def back_copy(zz, hi):
        return remote(
            back.at[zz, hi], grads.at[:, columns(hi, zz, c)], back_send.at[zz, hi], back_recv.at[zz, hi], sibling
        )

    def back_arrived(zz, hi):
        return remote(
            back.at[zz, hi], grads.at[:, columns(hi, zz, other)], back_send.at[zz, hi], back_recv.at[zz, hi], sibling
        )

    def back_of(rows, w):
        product = lax.dot_general(rows, w, (((1,), (1,)), ((), ())), preferred_element_type=F32)
        return (product * out_scale).astype(BF16)

    def multiply(zz):
        for hi in range(2):
            lower = [gathered[zz, :, 2 * hi + lo].reshape(block // 2, kw) for lo in range(2)]
            w = jnp.concatenate(lower, axis=0)
            back[zz, hi] = back_of(cot[tokens_of(other), :], w)
            back_copy(zz, hi).start()
            grads[:, columns(hi, zz, c)] = back_of(cot[tokens_of(c), :], w)
            keys[...] += jnp.dot(acts[zz, hi], w, preferred_element_type=F32)

    def cross_copy(h):
        return remote(
            cross_out.at[h], cross_in.at[h], cross_send.at[h], cross_recv.at[h], device(up(x, 2, NX), y, z, c)
        )

    def chain_end(part):
        for way in range(2):
            for k in (5, 6):
                chain_copy(way, k, part).wait_recv()
        for h in range(2):
            done = share(h, z, x_hi if part else 1 - x_hi)
            done += chain_in[0, 6 - h, part].astype(F32) + chain_in[1, 5 + h, part].astype(F32)
            if part:
                cross_own[h] = done
            else:
                cross_out[h] = done.astype(BF16)
                cross_copy(h).start()

    def outer_results():
        for j in range(GROUPS):
            @pl.when(g != j)
            def _():
                total_arrived(j).wait_recv()

        for j in range(GROUPS):
            own = pl.ds(j * piece, piece)
            weights_out[own, :], moved_out[own, :] = nesterov(total[j], master[own, :], momentum[own, :])

    def steps_near(i):
        for j in (2 * i - 1, 2 * i):
            @pl.when(j < NZ)
            def _():
                zz = wave(j)
                z_arrived(zz).wait_recv()

                @pl.when(jnp.logical_and(lax.rem(j, 2) == 1, j < 7))
                def _():
                    z_copy(zz, 1).start()

                @pl.when(jnp.logical_and(lax.rem(j, 2) == 0, j < 6))
                def _():
                    z_copy(zz, 0).start()

                stage_near(j, zz)

    def steps_line(i):
        @pl.when(jnp.logical_and(i >= LAG_Y + LINE_EARLY, i < NZ + LAG_Y))
        def _():
            stage_line(i - LAG_Y, wave(i - LAG_Y))

    def steps_far(i):
        @pl.when(jnp.logical_and(i >= LAG_F, i < NZ + LAG_F))
        def _():
            stage_far(i - LAG_F, wave(i - LAG_F))

    def steps_last(i):
        @pl.when(i >= LAG_END)
        def _():
            zz = wave(i - LAG_END)
            stage_last(i - LAG_END, zz)
            multiply(zz)

    def steps_first(i):
        @pl.when(i < 6)
        def _():
            first(i + 2)

    def steps_chain(i):
        @pl.when(i < 6)
        def _():
            chain(i + 1, False)

        for part in range(2):
            @pl.when(i == 7 + part)
            def _():
                chain_end(part)

    def steps_row(i):
        @pl.when(i == 1)
        def _():
            first_copy(far(0)).wait_recv()
            line(0, True)

        @pl.when(i == 2)
        def _():
            first_copy(far(1)).wait_recv()
            first_copy(far(2)).wait_recv()
            line(1, True)

        @pl.when(jnp.logical_or(i == 4, i == 6))
        def _():
            first_copy(far(i - 1)).wait_recv()
            first_copy(far(i)).wait_recv()

        @pl.when(jnp.logical_and(i >= 3, i < 8))
        def _():
            line(i - 1, False)

        @pl.when(i == 9)
        def _():
            line_end()

    def steps_total(i):
        @pl.when(i == TOTAL_AT)
        def _():
            @pl.loop(1, GROUPS)
            def _(d):
                total_copy(d).start()

        @pl.when(i == TOTAL_AT + 3)
        def _():
            outer_results()

    steps = {
        "near": steps_near, "line": steps_line, "far": steps_far, "last": steps_last,
        "first": steps_first, "chain": steps_chain, "row": steps_row, "total": steps_total,
    }
    if LINE_EARLY:
        stage_line(0, z)

    @pl.loop(1, NZ + LAG_END)
    def _(i):
        for name in ORDER:
            steps[name](i)

    keys_copy = remote(keys.at[tokens_of(other)], keys_in, pair_send.at[1], pair_recv.at[1], sibling)
    keys_copy.start()

    for h in range(2):
        cross_copy(h).wait_recv()
        wgrad_out[pl.ds(h * half, late), :] = (cross_own[h] + cross_in[h].astype(F32)) * out_scale

    keys_copy.wait_recv()
    keys_out[...] = ((keys[tokens_of(c), :] + keys_in[...]) * out_scale).astype(BF16)

    cot_swap.wait_send()
    cot_t_swap.wait_send()
    keys_copy.wait_send()
    for h in range(2):
        cross_copy(h).wait_send()

    @pl.loop(0, NZ)
    def _(zz):
        for hi in range(2):
            act_swap(zz, hi).wait_send()
            back_copy(zz, hi).wait_send()
            back_arrived(zz, hi).wait_recv()
        first_copy(zz).wait_send()
        stage_sent(zz, wave(zz))

    @pl.loop(0, 4)
    def _(d):
        z_copy(up(z, d, NZ), 1).wait_send()

    @pl.loop(0, 3)
    def _(d):
        z_copy(up(z, NZ - d, NZ), 0).wait_send()

    @pl.loop(1, NZ)
    def _(d):
        coded_copy(d).wait_send()
        total_copy(d).wait_send()
        for way in range(2):
            for part in range(2):
                chain_copy(way, d - 1, part).wait_send()
            line_copy(way, d - 1).wait_send()


def finish(weights, moved, keys, grads, turned, weights_hbm, moved_hbm, keys_hbm, grads_hbm, wgrad_hbm, wgrad, sem):
    pairs = ((grads, grads_hbm), (weights, weights_hbm), (moved, moved_hbm), (keys, keys_hbm), (wgrad, wgrad_hbm))
    copies = [pltpu.make_async_copy(src, dst, sem.at[i]) for i, (src, dst) in enumerate(pairs)]
    for copy in copies[:4]:
        copy.start()
    wgrad[...] = turned[...].T
    copies[4].start()
    for copy in copies:
        copy.wait()


def body(delta_codes, master_weights, outer_momentum, activations, key_cotangent):
    tokens, width = activations.shape
    rows, kw = master_weights.shape
    block, piece, half = width // 32, width // 32 // GROUPS, kw // 2
    late = half - CROSS_FIRST
    dma = pltpu.SemaphoreType.DMA
    hbm = pl.BlockSpec(memory_space=pl.ANY)
    vmem = pl.BlockSpec(memory_space=pltpu.VMEM)
    arguments = (delta_codes[0], master_weights, outer_momentum, activations, key_cotangent)
    results = pl.pallas_call(
        kernel,
        name="outer_step",
        out_shape=(
            pltpu.VMEM((rows, kw), F32),
            pltpu.VMEM((rows, kw), F32),
            pltpu.VMEM((tokens, kw), BF16),
            pltpu.VMEM((tokens, width), BF16),
            pltpu.VMEM((kw, block), F32),
        ),
        in_specs=[hbm] * 5,
        out_specs=(vmem,) * 5,
        scratch_shapes=[
            pltpu.VMEM((rows, kw), jnp.int32),
            pltpu.VMEM((rows, kw), F32),
            pltpu.VMEM((rows, kw), F32),
            pltpu.VMEM((2 * tokens, kw), BF16),
            pltpu.VMEM((2, 2, half, tokens), BF16),
            pltpu.VMEM((2, late, 2 * tokens), BF16),
            pltpu.VMEM((2, CROSS_FIRST, 2 * tokens), BF16),
            pltpu.VMEM((NZ, 2, 2 * tokens, block), BF16),
            pltpu.VMEM((GROUPS, piece, kw), BF16),
            pltpu.VMEM((GROUPS, piece, kw), BF16),
            pltpu.VMEM((GROUPS, piece, kw), BF16),
            pltpu.VMEM((NZ, NY, NX, piece, kw), BF16),
            pltpu.VMEM((2, 7, 2, late, block), BF16),
            pltpu.VMEM((2, 7, 2, late, block), BF16),
            pltpu.VMEM((2, late, block), BF16),
            pltpu.VMEM((2, late, block), BF16),
            pltpu.VMEM((2, late, block), F32),
            pltpu.VMEM((NZ, 2, CROSS_FIRST, block), BF16),
            pltpu.VMEM((NZ, 2, CROSS_FIRST, block), BF16),
            pltpu.VMEM((2, 7, CROSS_FIRST, block), BF16),
            pltpu.VMEM((2, 7, CROSS_FIRST, block), BF16),
            pltpu.VMEM((2 * tokens, kw), F32),
            pltpu.VMEM((tokens, kw), F32),
            pltpu.VMEM((NZ, 2, tokens, block), BF16),
            dma((4,)),
            dma((NZ, 2)),
            dma((NZ, 2)),
            dma((NZ, 2)),
            dma((3,)),
            dma((3,)),
            dma((GROUPS,)),
            dma((GROUPS,)),
            dma((GROUPS,)),
            dma((GROUPS,)),
            dma((NZ, 2)),
            dma((NZ,)),
            dma((NZ, NX)),
            dma((NZ, NX)),
            dma((NZ, 2)),
            dma((NZ, 2)),
            dma((NZ, 2)),
            dma((NZ, 2)),
            dma((2, 7, 2)),
            dma((2, 7, 2)),
            dma((2,)),
            dma((2,)),
            dma((NZ,)),
            dma((NZ,)),
            dma((2, 7)),
            dma((2, 7)),
            dma((NZ, 2)),
            dma((NZ, 2)),
        ],
        compiler_params=pltpu.CompilerParams(
            collective_id=0, has_side_effects=True, vmem_limit_bytes=44 * 2**20
        ),
        cost_estimate=pl.CostEstimate(
            flops=6 * tokens * width * kw, bytes_accessed=16 * 2**20, transcendentals=0
        ),
    )(*[pltpu.with_memory_space_constraint(a, pltpu.HBM) for a in arguments])
    weights, moved, keys, grads, wgrad = pl.pallas_call(
        finish,
        name="finish",
        out_shape=(
            jax.ShapeDtypeStruct((rows, kw), F32),
            jax.ShapeDtypeStruct((rows, kw), F32),
            jax.ShapeDtypeStruct((tokens, kw), BF16),
            jax.ShapeDtypeStruct((tokens, width), BF16),
            jax.ShapeDtypeStruct((rows, kw), F32),
        ),
        in_specs=[vmem] * 5,
        out_specs=(hbm,) * 5,
        scratch_shapes=[pltpu.VMEM((rows, kw), F32), dma((5,))],
        compiler_params=pltpu.CompilerParams(vmem_limit_bytes=16 * 2**20),
    )(*[pltpu.with_memory_space_constraint(r, pltpu.VMEM) for r in results])
    return weights, moved, keys, grads, wgrad[None]


def solution(mesh):
    placed = (
        P("group", "fsdp", None),
        P("fsdp", None),
        P("fsdp", None),
        P(("group", "fsdp"), None),
        P(("group", "fsdp"), None),
    )
    return jax.shard_map(
        body,
        mesh=mesh,
        in_specs=placed,
        out_specs=(
            P("fsdp", None),
            P("fsdp", None),
            P(("group", "fsdp"), None),
            P(("group", "fsdp"), None),
            P("group", "fsdp", None),
        ),
        check_vma=False,
    )
```

```python
import functools

import jax
import jax.numpy as jnp
from jax import lax
from jax.experimental import pallas as pl
from jax.experimental.pallas import tpu as pltpu
from jax.sharding import PartitionSpec as P

MESH = pl.DeviceIdType.MESH
F32 = jnp.float32
BF16 = jnp.bfloat16
NX, NY, NZ = 4, 4, 8
GROUPS = 8
LAG_Y, LAG_F, LAG_END = 1, 3, 5
LINE_EARLY = 0
TOTAL_AT = 6
ORDER = ("near", "line", "total", "row", "far", "first", "last", "chain")
CROSS_FIRST = 96
TURNED = (4, 6)


def device(x, y, z, c):
    return (lax.rem(x, 2) * 4 + y, lax.div(x, 2) * 16 + z * 2 + c)


def up(v, d, n):
    return lax.rem(v + d, n)


def dequantize(codes):
    values = codes.astype(F32)
    size = jnp.abs(values)
    largest = jnp.max(size, axis=-1, keepdims=True)
    scale = jnp.floor((largest + 0.5) / 127.0) + 1.0
    half = jnp.floor(scale * 0.5)
    magnitude = jnp.floor((size + half + 0.5) / scale)
    signed = jnp.where(values < 0.0, -magnitude, magnitude)
    return signed * scale * (1.0 / 4096.0)


def nesterov(total, weights, momentum):
    outer_grad = total.astype(F32) / GROUPS
    moved = 0.9 * momentum + outer_grad
    return weights - 0.7 * (outer_grad + 0.9 * moved), moved


def kernel(
    delta_hbm, master_hbm, momentum_hbm, acts_hbm, cot_hbm,
    weights_out, moved_out, keys_out, grads, wgrad_out,
    delta, master, momentum, cot, cot_t, late_t, early_t, acts,
    coded, coded_in, total, gathered,
    chain_out, chain_in, cross_out, cross_in, cross_own,
    first_out, first_in, line_out, line_in,
    keys, keys_in, back,
    load_sem, acts_load, acts_send, acts_recv, pair_send, pair_recv,
    coded_send, coded_recv, total_send, total_recv,
    z_send, z_recv, x_send, x_recv, y_send, y_recv, f_send, f_recv,
    chain_send, chain_recv, cross_send, cross_recv,
    first_send, first_recv, line_send, line_recv,
    back_send, back_recv,
):
    tokens, width = acts_hbm.shape
    kw = cot_hbm.shape[1]
    block = width // 32
    piece = block // GROUPS
    half = kw // 2
    late = half - CROSS_FIRST
    out_scale = width ** (-0.5)

    g, f = lax.axis_index("group"), lax.axis_index("fsdp")
    y, x_lo = lax.rem(g, NY), lax.div(g, NY)
    c, z, x_hi = lax.rem(f, 2), lax.rem(lax.div(f, 2), NZ), lax.div(f, 16)
    x = 2 * x_hi + x_lo
    other = 1 - c
    sibling = device(x, y, z, other)
    along_z = [device(x, y, up(z, d, NZ), c) for d in (1, NZ - 1)]
    along_x = [device(up(x, d, NX), y, z, c) for d in range(NX)]
    along_y = [device(x, up(y, d, NY), z, c) for d in range(NY)]
    pair_x = 2 * x_hi + 1 - x_lo
    pair_y = [device(pair_x, up(y, d, NY), z, c) for d in range(NY)]

    def member(j):
        return device(2 * x_hi + lax.div(j, NY), lax.rem(j, NY), z, c)

    def remote(src, dst, send, recv, to):
        return pltpu.make_async_remote_copy(
            src_ref=src, dst_ref=dst, send_sem=send, recv_sem=recv, device_id=to, device_id_type=MESH
        )

    def columns(hi, zz, core):
        return pl.ds(pl.multiple_of((hi * 16 + zz * 2 + core) * block, block), block)

    def tokens_of(core):
        return pl.ds(pl.multiple_of(core * tokens, tokens), tokens)

    def act_load(zz, hi):
        return pltpu.make_async_copy(
            acts_hbm.at[:, columns(hi, zz, c)], acts.at[zz, hi, tokens_of(c)], acts_load.at[zz, hi]
        )

    def act_swap(zz, hi):
        return remote(
            acts_hbm.at[:, columns(hi, zz, other)], acts.at[zz, hi, tokens_of(c)],
            acts_send.at[0], acts_recv.at[zz, hi], sibling,
        )

    def act_arrived(zz, hi):
        return remote(
            acts_hbm.at[:, columns(hi, zz, other)], acts.at[zz, hi, tokens_of(other)],
            acts_send.at[0], acts_recv.at[zz, hi], sibling,
        )

    def far(i):
        step = lax.div(i + 1, 2)
        return lax.rem(z + 4 + step * (2 * lax.rem(i, 2) - 1) * -1 + NZ, NZ)

    loads = [
        pltpu.make_async_copy(delta_hbm, delta, load_sem.at[0]),
        pltpu.make_async_copy(cot_hbm, cot.at[tokens_of(c)], load_sem.at[1]),
        pltpu.make_async_copy(master_hbm, master, load_sem.at[2]),
        pltpu.make_async_copy(momentum_hbm, momentum, load_sem.at[3]),
    ]
    loads[0].start()

    partners = [sibling] + along_z + along_x[1:] + along_y[1:] + pair_y[1:]
    barrier = pltpu.get_barrier_semaphore()
    for partner in partners:
        pl.semaphore_signal(barrier, inc=1, device_id=partner, device_id_type=MESH)
    for load in loads[1:]:
        load.start()
    for hi in range(2):
        act_load(far(0), hi).start()

    loads[0].wait()
    for j in range(GROUPS):
        for k in range(kw // 128):
            codes = delta[pl.ds(j * piece, piece), pl.ds(k * 128, 128)]
            coded[j, :, pl.ds(k * 128, 128)] = dequantize(codes).astype(BF16)
    loads[1].wait()
    cot_t[c] = cot[tokens_of(c), :].T.reshape(2, half, tokens)
    pl.semaphore_wait(barrier, len(partners))

    def coded_copy(d):
        j = up(g, d, GROUPS)
        return remote(coded.at[j], coded_in.at[g], coded_send.at[0], coded_recv.at[g], member(j))

    def coded_arrived(j):
        return remote(coded.at[j], coded_in.at[j], coded_send.at[0], coded_recv.at[j], sibling)

    @pl.loop(1, GROUPS)
    def _(d):
        coded_copy(d).start()

    cot_t_swap = remote(cot_t.at[c], cot_t.at[c], pair_send.at[2], pair_recv.at[2], sibling)
    cot_t_swap.start()

    for hi in range(2):
        act_swap(far(0), hi).start()
    cot_swap = remote(cot_hbm, cot.at[tokens_of(c)], pair_send.at[0], pair_recv.at[0], sibling)
    cot_swap.start()

    @pl.loop(1, NZ)
    def _(i):
        for hi in range(2):
            act_swap(far(i), hi).start()
            act_load(far(i), hi).start()


    def acts_ready(zz):
        for hi in range(2):
            act_load(zz, hi).wait()
            act_arrived(zz, hi).wait_recv()

    def chain_copy(way, k, part):
        return remote(
            chain_out.at[way, k, part], chain_in.at[way, k, part],
            chain_send.at[0], chain_recv.at[way, k, part], along_z[way],
        )

    def share(h, zz, hi):
        return jnp.dot(late_t[h], acts[zz, hi], preferred_element_type=F32)

    def early_share(h, zz, hi):
        return jnp.dot(early_t[h], acts[zz, hi], preferred_element_type=F32)

    def first_copy(zz):
        return remote(
            first_out.at[zz], first_in.at[zz], first_send.at[0], first_recv.at[zz], along_x[2]
        )

    def first(i):
        zz = far(i)
        for h in range(2):
            first_out[zz, h] = early_share(h, zz, 1 - x_hi).astype(BF16)
        first_copy(zz).start()

    def line_copy(way, k):
        return remote(line_out.at[way, k], line_in.at[way, k], line_send.at[0], line_recv.at[way, k], along_z[way])

    def line(k, opening):
        s = lax.div(k + 1, 2)
        for way in range(2):
            zz = up(z, 4 - s if way == 0 else 4 + s, NZ)
            h = lax.rem(k + way, 2)
            if not opening:
                line_copy(way, k - 2).wait_recv()
            sent = early_share(h, zz, x_hi) + first_in[zz, h].astype(F32)
            if not opening:
                sent += line_in[way, k - 2].astype(F32)
            line_out[way, k] = sent.astype(BF16)
            line_copy(way, k).start()

    def line_end():
        first_copy(z).wait_recv()
        for way in range(2):
            for k in (5, 6):
                line_copy(way, k).wait_recv()
        for h in range(2):
            done = early_share(h, z, x_hi) + first_in[z, h].astype(F32)
            done += line_in[0, 6 - h].astype(F32) + line_in[1, 5 + h].astype(F32)
            wgrad_out[pl.ds(h * half + late, CROSS_FIRST), :] = done * out_scale

    def chain(k, opening):
        s = lax.div(k + 1, 2)
        for part in range(2):
            for way in range(2):
                zz = up(z, 4 - s if way == 0 else 4 + s, NZ)
                h = lax.rem(k + way, 2)
                sent = share(h, zz, x_hi if part else 1 - x_hi)
                if not opening:
                    chain_copy(way, k - 2, part).wait_recv()
                    sent += chain_in[way, k - 2, part].astype(F32)
                chain_out[way, k, part] = sent.astype(BF16)
                chain_copy(way, k, part).start()

    remote(cot_t.at[other], cot_t.at[other], pair_send.at[2], pair_recv.at[2], sibling).wait_recv()
    for h in range(2):
        for core in range(2):
            late_t[h, :, pl.ds(core * tokens, tokens)] = cot_t[core, h, :late]
            early_t[h, :, pl.ds(core * tokens, tokens)] = cot_t[core, h, late:]
    acts_ready(far(0))
    chain(0, True)
    first(0)

    rows = pl.ds(pl.multiple_of(g * piece, piece), piece)

    @pl.loop(1, GROUPS)
    def _(d):
        coded_arrived(up(g, d, GROUPS)).wait_recv()

    summed = coded[g].astype(F32)
    for d in range(1, GROUPS):
        summed += coded_in[up(g, d, GROUPS)].astype(F32)
    total[g] = summed.astype(BF16)
    loads[2].wait()
    loads[3].wait()
    updated, _ = nesterov(total[g], master[rows, :], momentum[rows, :])
    gathered[z, y, x] = updated.astype(BF16)

    def z_copy(zz, way):
        return remote(gathered.at[zz, y, x], gathered.at[zz, y, x], z_send.at[0], z_recv.at[zz], along_z[way])

    def z_arrived(zz):
        return remote(gathered.at[zz, y, x], gathered.at[zz, y, x], z_send.at[0], z_recv.at[zz], sibling)

    def near_copy(zz, d, turned):
        to = along_y[d] if turned else along_x[d]
        part = gathered.at[zz, y, x]
        return remote(part, part, x_send.at[0], x_recv.at[zz, y if turned else x], to)

    def near_arrived(zz, d, turned):
        at = up(y if turned else x, d, NX)
        part = gathered.at[zz, at, x] if turned else gathered.at[zz, y, at]
        return remote(part, part, x_send.at[0], x_recv.at[zz, at], sibling)

    def neighbour(way, turned):
        d = 1 if way == 0 else NX - 1
        return along_x[d] if turned else along_y[d]

    def line_of(zz, d, turned):
        return gathered.at[zz, :, up(x, d, NX)] if turned else gathered.at[zz, up(y, d, NY)]

    def half_of(zz, d, way, turned):
        if turned:
            return gathered.at[zz, pl.ds(way * 2, 2), up(x, d, NX)]
        return gathered.at[zz, up(y, d, NY), pl.ds(way * 2, 2)]

    def y_copy(zz, way, turned):
        part = line_of(zz, 0, turned)
        return remote(part, part, y_send.at[0], y_recv.at[zz, way], neighbour(way, turned))

    def y_arrived(zz, way, turned):
        part = line_of(zz, 3 if way == 0 else 1, turned)
        return remote(part, part, y_send.at[0], y_recv.at[zz, way], sibling)

    def f_copy(zz, way, turned):
        part = half_of(zz, 3 if way == 0 else 1, way, turned)
        return remote(part, part, f_send.at[0], f_recv.at[zz, way], neighbour(way, turned))

    def f_arrived(zz, way, turned):
        part = half_of(zz, 2, way, turned)
        return remote(part, part, f_send.at[0], f_recv.at[zz, way], sibling)

    def either(i, step):
        if isinstance(i, int):
            step(i in TURNED)
            return
        hit = i == -1
        for t in TURNED:
            hit = jnp.logical_or(hit, i == t)
        pl.when(hit)(lambda: step(True))
        pl.when(jnp.logical_not(hit))(lambda: step(False))

    def stage_near(i, zz):
        def step(turned):
            for d in range(1, NX):
                near_copy(zz, d, turned).start()

        either(i, step)

    def stage_line(i, zz):
        def step(turned):
            for d in range(1, NX):
                near_arrived(zz, d, turned).wait_recv()
            for way in range(2):
                y_copy(zz, way, turned).start()

        either(i, step)

    def stage_far(i, zz):
        def step(turned):
            for way in range(2):
                y_arrived(zz, way, turned).wait_recv()
            for way in range(2):
                f_copy(zz, way, turned).start()

        either(i, step)

    def stage_last(i, zz):
        def step(turned):
            for way in range(2):
                f_arrived(zz, way, turned).wait_recv()

        either(i, step)

    for way in range(2):
        z_copy(z, way).start()
    stage_near(0, z)

    def total_copy(j, to):
        return remote(total.at[j], total.at[j], total_send.at[0], total_recv.at[j], to)

    pair_g = up(g, NY, GROUPS)

    acts_ready(far(1))
    acts_ready(far(2))
    chain(1, True)
    first(1)
    first(2)
    remote(cot_hbm, cot.at[tokens_of(other)], pair_send.at[0], pair_recv.at[0], sibling).wait_recv()

    @pl.loop(3, NZ)
    def _(i):
        acts_ready(far(i))

    def wave(i):
        return lax.rem(z + lax.div(i + 1, 2) * (2 * lax.rem(i, 2) - 1) + NZ, NZ)

    keys[...] = jnp.zeros_like(keys)

    def back_copy(zz, hi):
        return remote(
            back.at[zz, hi], grads.at[:, columns(hi, zz, c)], back_send.at[0], back_recv.at[0], sibling
        )

    def back_arrived(zz, hi):
        return remote(
            back.at[zz, hi], grads.at[:, columns(hi, zz, other)], back_send.at[0], back_recv.at[0], sibling
        )

    def back_of(rows, w):
        product = lax.dot_general(rows, w, (((1,), (1,)), ((), ())), preferred_element_type=F32)
        return (product * out_scale).astype(BF16)

    keys_copy = remote(keys.at[tokens_of(other)], keys_in, pair_send.at[1], pair_recv.at[1], sibling)

    def multiply(zz, last):
        parts = [gathered[zz, :, xx].reshape(block // 2, kw) for xx in range(NX)]
        w = jnp.concatenate(parts, axis=0)
        both = jnp.concatenate([acts[zz, hi] for hi in range(2)], axis=1)
        keys[...] += jnp.dot(both, w, preferred_element_type=F32)

        @pl.when(last)
        def _():
            keys_copy.start()

        for hi in range(2):
            half_w = jnp.concatenate(parts[2 * hi : 2 * hi + 2], axis=0)
            back[zz, hi] = back_of(cot[tokens_of(other), :], half_w)
            back_copy(zz, hi).start()
        for hi in range(2):
            half_w = jnp.concatenate(parts[2 * hi : 2 * hi + 2], axis=0)
            grads[:, columns(hi, zz, c)] = back_of(cot[tokens_of(c), :], half_w)

    def cross_copy(h):
        return remote(
            cross_out.at[h], cross_in.at[h], cross_send.at[0], cross_recv.at[h], along_x[2]
        )

    def chain_end(part):
        for way in range(2):
            for k in (5, 6):
                chain_copy(way, k, part).wait_recv()
        for h in range(2):
            done = share(h, z, x_hi if part else 1 - x_hi)
            done += chain_in[0, 6 - h, part].astype(F32) + chain_in[1, 5 + h, part].astype(F32)
            if part:
                cross_own[h] = done
            else:
                cross_out[h] = done.astype(BF16)
                cross_copy(h).start()

    def outer_results():
        @pl.loop(1, NY)
        def _(d):
            for lo in range(2):
                total_copy(lo * NY + up(y, d, NY), sibling).wait_recv()

        for j in range(GROUPS):
            own = pl.ds(j * piece, piece)
            weights_out[own, :], moved_out[own, :] = nesterov(total[j], master[own, :], momentum[own, :])

    def steps_near(i):
        for j in (2 * i - 1, 2 * i):
            @pl.when(j < NZ)
            def _():
                zz = wave(j)
                z_arrived(zz).wait_recv()

                @pl.when(jnp.logical_and(lax.rem(j, 2) == 1, j < 7))
                def _():
                    z_copy(zz, 1).start()

                @pl.when(jnp.logical_and(lax.rem(j, 2) == 0, j < 6))
                def _():
                    z_copy(zz, 0).start()

                stage_near(j, zz)

    def steps_line(i):
        @pl.when(jnp.logical_and(i >= LAG_Y + LINE_EARLY, i < NZ + LAG_Y))
        def _():
            stage_line(i - LAG_Y, wave(i - LAG_Y))

    def steps_far(i):
        @pl.when(jnp.logical_and(i >= LAG_F, i < NZ + LAG_F))
        def _():
            stage_far(i - LAG_F, wave(i - LAG_F))

    def steps_last(i):
        @pl.when(i >= LAG_END)
        def _():
            zz = wave(i - LAG_END)
            stage_last(i - LAG_END, zz)
            multiply(zz, i == NZ + LAG_END - 1)

    def steps_first(i):
        @pl.when(i < 6)
        def _():
            first(i + 2)

    def steps_chain(i):
        @pl.when(i < 6)
        def _():
            chain(i + 1, False)

        for part in range(2):
            @pl.when(i == 7 + part)
            def _():
                chain_end(part)

    def steps_row(i):
        @pl.when(i == 1)
        def _():
            first_copy(far(0)).wait_recv()
            line(0, True)

        @pl.when(i == 2)
        def _():
            first_copy(far(1)).wait_recv()
            first_copy(far(2)).wait_recv()
            line(1, True)

        @pl.when(jnp.logical_or(i == 4, i == 6))
        def _():
            first_copy(far(i - 1)).wait_recv()
            first_copy(far(i)).wait_recv()

        @pl.when(jnp.logical_and(i >= 3, i < 8))
        def _():
            line(i - 1, False)

        @pl.when(i == 9)
        def _():
            line_end()

    def steps_total(i):
        @pl.when(i == TOTAL_AT)
        def _():
            total_copy(g, pair_y[0]).start()

        @pl.when(i == TOTAL_AT + 1)
        def _():
            total_copy(pair_g, sibling).wait_recv()
            for d in range(1, NY):
                total_copy(g, along_y[d]).start()
                total_copy(pair_g, along_y[d]).start()

        @pl.when(i == TOTAL_AT + 4)
        def _():
            outer_results()

    steps = {
        "near": steps_near, "line": steps_line, "far": steps_far, "last": steps_last,
        "first": steps_first, "chain": steps_chain, "row": steps_row, "total": steps_total,
    }
    if LINE_EARLY:
        stage_line(0, z)

    @pl.loop(1, NZ + LAG_END)
    def _(i):
        for name in ORDER:
            steps[name](i)

    for h in range(2):
        cross_copy(h).wait_recv()
        wgrad_out[pl.ds(h * half, late), :] = (cross_own[h] + cross_in[h].astype(F32)) * out_scale

    keys_copy.wait_recv()
    keys_out[...] = ((keys[tokens_of(c), :] + keys_in[...]) * out_scale).astype(BF16)

    cot_swap.wait_send()
    cot_t_swap.wait_send()
    keys_copy.wait_send()
    for part, sem in (
        (coded.at[pl.ds(0, 7)], coded_send),
        (total.at[pl.ds(0, 7)], total_send),
        (gathered.at[pl.ds(0, 7), 0, 0], z_send),
        (gathered.at[pl.ds(0, 6), 0], x_send),
        (gathered.at[pl.ds(0, 4)], y_send),
        (gathered.at[pl.ds(0, 2)], f_send),
        (chain_out, chain_send),
        (line_out, line_send),
        (first_out, first_send),
        (cross_out, cross_send),
        (back, acts_send),
        (back, back_send),
    ):
        remote(part, part, sem.at[0], pair_recv.at[1], sibling).wait_send()
    remote(back, back, back_send.at[0], back_recv.at[0], sibling).wait_recv()


def finish(weights, moved, keys, grads, turned, weights_hbm, moved_hbm, keys_hbm, grads_hbm, wgrad_hbm, wgrad, sem):
    pairs = ((grads, grads_hbm), (weights, weights_hbm), (moved, moved_hbm), (keys, keys_hbm), (wgrad, wgrad_hbm))
    copies = [pltpu.make_async_copy(src, dst, sem.at[i]) for i, (src, dst) in enumerate(pairs)]
    for copy in copies[:4]:
        copy.start()
    wgrad[...] = turned[...].T
    copies[4].start()
    for copy in copies:
        copy.wait()


def body(delta_codes, master_weights, outer_momentum, activations, key_cotangent):
    tokens, width = activations.shape
    rows, kw = master_weights.shape
    block, piece, half = width // 32, width // 32 // GROUPS, kw // 2
    late = half - CROSS_FIRST
    dma = pltpu.SemaphoreType.DMA
    hbm = pl.BlockSpec(memory_space=pl.ANY)
    vmem = pl.BlockSpec(memory_space=pltpu.VMEM)
    arguments = (delta_codes[0], master_weights, outer_momentum, activations, key_cotangent)
    results = pl.pallas_call(
        kernel,
        name="outer_step",
        out_shape=(
            pltpu.VMEM((rows, kw), F32),
            pltpu.VMEM((rows, kw), F32),
            pltpu.VMEM((tokens, kw), BF16),
            pltpu.VMEM((tokens, width), BF16),
            pltpu.VMEM((kw, block), F32),
        ),
        in_specs=[hbm] * 5,
        out_specs=(vmem,) * 5,
        scratch_shapes=[
            pltpu.VMEM((rows, kw), jnp.int32),
            pltpu.VMEM((rows, kw), F32),
            pltpu.VMEM((rows, kw), F32),
            pltpu.VMEM((2 * tokens, kw), BF16),
            pltpu.VMEM((2, 2, half, tokens), BF16),
            pltpu.VMEM((2, late, 2 * tokens), BF16),
            pltpu.VMEM((2, CROSS_FIRST, 2 * tokens), BF16),
            pltpu.VMEM((NZ, 2, 2 * tokens, block), BF16),
            pltpu.VMEM((GROUPS, piece, kw), BF16),
            pltpu.VMEM((GROUPS, piece, kw), BF16),
            pltpu.VMEM((GROUPS, piece, kw), BF16),
            pltpu.VMEM((NZ, NY, NX, piece, kw), BF16),
            pltpu.VMEM((2, 7, 2, late, block), BF16),
            pltpu.VMEM((2, 7, 2, late, block), BF16),
            pltpu.VMEM((2, late, block), BF16),
            pltpu.VMEM((2, late, block), BF16),
            pltpu.VMEM((2, late, block), F32),
            pltpu.VMEM((NZ, 2, CROSS_FIRST, block), BF16),
            pltpu.VMEM((NZ, 2, CROSS_FIRST, block), BF16),
            pltpu.VMEM((2, 7, CROSS_FIRST, block), BF16),
            pltpu.VMEM((2, 7, CROSS_FIRST, block), BF16),
            pltpu.VMEM((2 * tokens, kw), F32),
            pltpu.VMEM((tokens, kw), F32),
            pltpu.VMEM((NZ, 2, tokens, block), BF16),
            dma((4,)),
            dma((NZ, 2)),
            dma((1,)),
            dma((NZ, 2)),
            dma((3,)),
            dma((3,)),
            dma((1,)),
            dma((GROUPS,)),
            dma((1,)),
            dma((GROUPS,)),
            dma((1,)),
            dma((NZ,)),
            dma((1,)),
            dma((NZ, NX)),
            dma((1,)),
            dma((NZ, 2)),
            dma((1,)),
            dma((NZ, 2)),
            dma((1,)),
            dma((2, 7, 2)),
            dma((1,)),
            dma((2,)),
            dma((1,)),
            dma((NZ,)),
            dma((1,)),
            dma((2, 7)),
            dma((1,)),
            dma((1,)),
        ],
        compiler_params=pltpu.CompilerParams(
            collective_id=0, has_side_effects=True, vmem_limit_bytes=44 * 2**20
        ),
        cost_estimate=pl.CostEstimate(
            flops=6 * tokens * width * kw, bytes_accessed=16 * 2**20, transcendentals=0
        ),
    )(*[pltpu.with_memory_space_constraint(a, pltpu.HBM) for a in arguments])
    weights, moved, keys, grads, wgrad = pl.pallas_call(
        finish,
        name="finish",
        out_shape=(
            jax.ShapeDtypeStruct((rows, kw), F32),
            jax.ShapeDtypeStruct((rows, kw), F32),
            jax.ShapeDtypeStruct((tokens, kw), BF16),
            jax.ShapeDtypeStruct((tokens, width), BF16),
            jax.ShapeDtypeStruct((rows, kw), F32),
        ),
        in_specs=[vmem] * 5,
        out_specs=(hbm,) * 5,
        scratch_shapes=[pltpu.VMEM((rows, kw), F32), dma((5,))],
        compiler_params=pltpu.CompilerParams(vmem_limit_bytes=16 * 2**20),
    )(*[pltpu.with_memory_space_constraint(r, pltpu.VMEM) for r in results])
    return weights, moved, keys, grads, wgrad[None]


def solution(mesh):
    placed = (
        P("group", "fsdp", None),
        P("fsdp", None),
        P("fsdp", None),
        P(("group", "fsdp"), None),
        P(("group", "fsdp"), None),
    )
    return jax.shard_map(
        body,
        mesh=mesh,
        in_specs=placed,
        out_specs=(
            P("fsdp", None),
            P("fsdp", None),
            P(("group", "fsdp"), None),
            P(("group", "fsdp"), None),
            P("group", "fsdp", None),
        ),
        check_vma=False,
    )
```

```python
import functools

import jax
import jax.numpy as jnp
from jax import lax
from jax.experimental import pallas as pl
from jax.experimental.pallas import tpu as pltpu
from jax.sharding import PartitionSpec as P

MESH = pl.DeviceIdType.MESH
F32 = jnp.float32
BF16 = jnp.bfloat16
NX, NY, NZ = 4, 4, 8
GROUPS = 8
LAG_Y, LAG_F, LAG_END = 1, 3, 5
LINE_EARLY = 0
TOTAL_AT, TOTAL_ON, TOTAL_END = 4, 7, 11
NEAR_AT = (1, 1, 2, 2, 3, 3, 6)
ORDER = ("near", "line", "total", "row", "far", "first", "last", "chain")
CROSS_FIRST = 96
TURNED = (4, 6)


def device(x, y, z, c):
    return (lax.rem(x, 2) * 4 + y, lax.div(x, 2) * 16 + z * 2 + c)


def up(v, d, n):
    return lax.rem(v + d, n)


def dequantize(codes):
    values = codes.astype(F32)
    size = jnp.abs(values)
    largest = jnp.max(size, axis=-1, keepdims=True)
    scale = jnp.floor((largest + 0.5) / 127.0) + 1.0
    half = jnp.floor(scale * 0.5)
    magnitude = jnp.floor((size + half + 0.5) / scale)
    signed = jnp.where(values < 0.0, -magnitude, magnitude)
    return signed * scale * (1.0 / 4096.0)


def nesterov(total, weights, momentum):
    outer_grad = total.astype(F32) / GROUPS
    moved = 0.9 * momentum + outer_grad
    return weights - 0.7 * (outer_grad + 0.9 * moved), moved


def kernel(
    delta_hbm, master_hbm, momentum_hbm, acts_hbm, cot_hbm,
    weights_out, moved_out, keys_out, grads, wgrad_out,
    delta, master, momentum, cot, cot_t, late_t, early_t, acts,
    coded, coded_in, total, gathered,
    chain_out, chain_in, cross_out, cross_in, cross_own,
    first_out, first_in, line_out, line_in,
    keys, keys_in, back,
    load_sem, acts_load, acts_send, acts_recv, pair_send, pair_recv,
    coded_send, coded_recv, total_send, total_recv,
    z_send, z_recv, x_send, x_recv, y_send, y_recv, f_send, f_recv,
    chain_send, chain_recv, cross_send, cross_recv,
    first_send, first_recv, line_send, line_recv,
    back_send, back_recv,
):
    tokens, width = acts_hbm.shape
    kw = cot_hbm.shape[1]
    block = width // 32
    piece = block // GROUPS
    half = kw // 2
    late = half - CROSS_FIRST
    out_scale = width ** (-0.5)

    g, f = lax.axis_index("group"), lax.axis_index("fsdp")
    y, x_lo = lax.rem(g, NY), lax.div(g, NY)
    c, z, x_hi = lax.rem(f, 2), lax.rem(lax.div(f, 2), NZ), lax.div(f, 16)
    x = 2 * x_hi + x_lo
    other = 1 - c
    sibling = device(x, y, z, other)
    along_z = [device(x, y, up(z, d, NZ), c) for d in (1, NZ - 1)]
    along_x = [device(up(x, d, NX), y, z, c) for d in range(NX)]
    along_y = [device(x, up(y, d, NY), z, c) for d in range(NY)]
    pair_x = 2 * x_hi + 1 - x_lo
    pair_y = [device(pair_x, up(y, d, NY), z, c) for d in range(NY)]

    def member(j):
        return device(2 * x_hi + lax.div(j, NY), lax.rem(j, NY), z, c)

    def remote(src, dst, send, recv, to):
        return pltpu.make_async_remote_copy(
            src_ref=src, dst_ref=dst, send_sem=send, recv_sem=recv, device_id=to, device_id_type=MESH
        )

    def columns(hi, zz, core):
        return pl.ds(pl.multiple_of((hi * 16 + zz * 2 + core) * block, block), block)

    def tokens_of(core):
        return pl.ds(pl.multiple_of(core * tokens, tokens), tokens)

    def act_load(zz, hi):
        return pltpu.make_async_copy(
            acts_hbm.at[:, columns(hi, zz, c)], acts.at[zz, hi, tokens_of(c)], acts_load.at[zz, hi]
        )

    def act_swap(zz, hi):
        return remote(
            acts_hbm.at[:, columns(hi, zz, other)], acts.at[zz, hi, tokens_of(c)],
            acts_send.at[0], acts_recv.at[zz, hi], sibling,
        )

    def act_arrived(zz, hi):
        return remote(
            acts_hbm.at[:, columns(hi, zz, other)], acts.at[zz, hi, tokens_of(other)],
            acts_send.at[0], acts_recv.at[zz, hi], sibling,
        )

    def far(i):
        step = lax.div(i + 1, 2)
        return lax.rem(z + 4 + step * (2 * lax.rem(i, 2) - 1) * -1 + NZ, NZ)

    loads = [
        pltpu.make_async_copy(delta_hbm, delta, load_sem.at[0]),
        pltpu.make_async_copy(cot_hbm, cot.at[tokens_of(c)], load_sem.at[1]),
        pltpu.make_async_copy(master_hbm, master, load_sem.at[2]),
        pltpu.make_async_copy(momentum_hbm, momentum, load_sem.at[3]),
    ]
    loads[0].start()

    partners = [sibling] + along_z + along_x[1:] + along_y[1:] + pair_y[1:]
    barrier = pltpu.get_barrier_semaphore()
    for partner in partners:
        pl.semaphore_signal(barrier, inc=1, device_id=partner, device_id_type=MESH)
    for load in loads[1:]:
        load.start()
    for hi in range(2):
        act_load(far(0), hi).start()

    loads[0].wait()
    for j in range(GROUPS):
        for k in range(kw // 128):
            codes = delta[pl.ds(j * piece, piece), pl.ds(k * 128, 128)]
            coded[j, :, pl.ds(k * 128, 128)] = dequantize(codes).astype(BF16)
    pl.semaphore_wait(barrier, len(partners))

    def coded_copy(d):
        j = up(g, d, GROUPS)
        return remote(coded.at[j], coded_in.at[g], coded_send.at[0], coded_recv.at[g], member(j))

    def coded_arrived(j):
        return remote(coded.at[j], coded_in.at[j], coded_send.at[0], coded_recv.at[j], sibling)

    @pl.loop(1, GROUPS)
    def _(d):
        coded_copy(d).start()

    for hi in range(2):
        act_swap(far(0), hi).start()
    loads[1].wait()
    cot_t[c] = cot[tokens_of(c), :].T.reshape(2, half, tokens)
    cot_t_swap = remote(cot_t.at[c], cot_t.at[c], pair_send.at[2], pair_recv.at[2], sibling)
    cot_t_swap.start()

    cot_swap = remote(cot_hbm, cot.at[tokens_of(c)], pair_send.at[0], pair_recv.at[0], sibling)
    cot_swap.start()

    @pl.loop(1, NZ)
    def _(i):
        for hi in range(2):
            act_swap(far(i), hi).start()
            act_load(far(i), hi).start()


    def acts_ready(zz):
        for hi in range(2):
            act_load(zz, hi).wait()
            act_arrived(zz, hi).wait_recv()

    def chain_copy(way, k, part):
        return remote(
            chain_out.at[way, k, part], chain_in.at[way, k, part],
            chain_send.at[0], chain_recv.at[way, k, part], along_z[way],
        )

    def share(h, zz, hi):
        return jnp.dot(late_t[h], acts[zz, hi], preferred_element_type=F32)

    def early_share(h, zz, hi):
        return jnp.dot(early_t[h], acts[zz, hi], preferred_element_type=F32)

    def first_copy(zz):
        return remote(
            first_out.at[zz], first_in.at[zz], first_send.at[0], first_recv.at[zz], along_x[2]
        )

    def first(i):
        zz = far(i)
        for h in range(2):
            first_out[zz, h] = early_share(h, zz, 1 - x_hi).astype(BF16)
        first_copy(zz).start()

    def line_copy(way, k):
        return remote(line_out.at[way, k], line_in.at[way, k], line_send.at[0], line_recv.at[way, k], along_z[way])

    def line(k, opening):
        s = lax.div(k + 1, 2)
        for way in range(2):
            zz = up(z, 4 - s if way == 0 else 4 + s, NZ)
            h = lax.rem(k + way, 2)
            if not opening:
                line_copy(way, k - 2).wait_recv()
            sent = early_share(h, zz, x_hi) + first_in[zz, h].astype(F32)
            if not opening:
                sent += line_in[way, k - 2].astype(F32)
            line_out[way, k] = sent.astype(BF16)
            line_copy(way, k).start()

    def line_end():
        first_copy(z).wait_recv()
        for way in range(2):
            for k in (5, 6):
                line_copy(way, k).wait_recv()
        for h in range(2):
            done = early_share(h, z, x_hi) + first_in[z, h].astype(F32)
            done += line_in[0, 6 - h].astype(F32) + line_in[1, 5 + h].astype(F32)
            wgrad_out[pl.ds(h * half + late, CROSS_FIRST), :] = done * out_scale

    def chain(k, opening):
        s = lax.div(k + 1, 2)
        for part in range(2):
            for way in range(2):
                zz = up(z, 4 - s if way == 0 else 4 + s, NZ)
                h = lax.rem(k + way, 2)
                sent = share(h, zz, x_hi if part else 1 - x_hi)
                if not opening:
                    chain_copy(way, k - 2, part).wait_recv()
                    sent += chain_in[way, k - 2, part].astype(F32)
                chain_out[way, k, part] = sent.astype(BF16)
                chain_copy(way, k, part).start()

    remote(cot_t.at[other], cot_t.at[other], pair_send.at[2], pair_recv.at[2], sibling).wait_recv()
    for h in range(2):
        for core in range(2):
            late_t[h, :, pl.ds(core * tokens, tokens)] = cot_t[core, h, :late]
            early_t[h, :, pl.ds(core * tokens, tokens)] = cot_t[core, h, late:]
    acts_ready(far(0))
    chain(0, True)
    first(0)

    rows = pl.ds(pl.multiple_of(g * piece, piece), piece)

    @pl.loop(1, GROUPS)
    def _(d):
        coded_arrived(up(g, d, GROUPS)).wait_recv()

    summed = coded[g].astype(F32)
    for d in range(1, GROUPS):
        summed += coded_in[up(g, d, GROUPS)].astype(F32)
    total[g] = summed.astype(BF16)
    loads[2].wait()
    loads[3].wait()
    updated, _ = nesterov(total[g], master[rows, :], momentum[rows, :])
    gathered[z, y, x] = updated.astype(BF16)

    def z_copy(zz, way):
        return remote(gathered.at[zz, y, x], gathered.at[zz, y, x], z_send.at[0], z_recv.at[zz], along_z[way])

    def z_arrived(zz):
        return remote(gathered.at[zz, y, x], gathered.at[zz, y, x], z_send.at[0], z_recv.at[zz], sibling)

    def near_copy(zz, d, turned):
        to = along_y[d] if turned else along_x[d]
        part = gathered.at[zz, y, x]
        return remote(part, part, x_send.at[0], x_recv.at[zz, y if turned else x], to)

    def near_arrived(zz, d, turned):
        at = up(y if turned else x, d, NX)
        part = gathered.at[zz, at, x] if turned else gathered.at[zz, y, at]
        return remote(part, part, x_send.at[0], x_recv.at[zz, at], sibling)

    def neighbour(way, turned):
        d = 1 if way == 0 else NX - 1
        return along_x[d] if turned else along_y[d]

    def line_of(zz, d, turned):
        return gathered.at[zz, :, up(x, d, NX)] if turned else gathered.at[zz, up(y, d, NY)]

    def half_of(zz, d, way, turned):
        if turned:
            return gathered.at[zz, pl.ds(way * 2, 2), up(x, d, NX)]
        return gathered.at[zz, up(y, d, NY), pl.ds(way * 2, 2)]

    def y_copy(zz, way, turned):
        part = line_of(zz, 0, turned)
        return remote(part, part, y_send.at[0], y_recv.at[zz, way], neighbour(way, turned))

    def y_arrived(zz, way, turned):
        part = line_of(zz, 3 if way == 0 else 1, turned)
        return remote(part, part, y_send.at[0], y_recv.at[zz, way], sibling)

    def f_copy(zz, way, turned):
        part = half_of(zz, 3 if way == 0 else 1, way, turned)
        return remote(part, part, f_send.at[0], f_recv.at[zz, way], neighbour(way, turned))

    def f_arrived(zz, way, turned):
        part = half_of(zz, 2, way, turned)
        return remote(part, part, f_send.at[0], f_recv.at[zz, way], sibling)

    def either(i, step):
        if isinstance(i, int):
            step(i in TURNED)
            return
        hit = i == -1
        for t in TURNED:
            hit = jnp.logical_or(hit, i == t)
        pl.when(hit)(lambda: step(True))
        pl.when(jnp.logical_not(hit))(lambda: step(False))

    def stage_near(i, zz):
        def step(turned):
            for d in range(1, NX):
                near_copy(zz, d, turned).start()

        either(i, step)

    def stage_line(i, zz):
        def step(turned):
            for d in range(1, NX):
                near_arrived(zz, d, turned).wait_recv()
            for way in range(2):
                y_copy(zz, way, turned).start()

        either(i, step)

    def stage_far(i, zz):
        def step(turned):
            for way in range(2):
                y_arrived(zz, way, turned).wait_recv()
            for way in range(2):
                f_copy(zz, way, turned).start()

        either(i, step)

    def stage_last(i, zz):
        def step(turned):
            for way in range(2):
                f_arrived(zz, way, turned).wait_recv()

        either(i, step)

    for way in range(2):
        z_copy(z, way).start()
    stage_near(0, z)

    def total_copy(j, to):
        return remote(total.at[j], total.at[j], total_send.at[0], total_recv.at[j], to)

    pair_g = up(g, NY, GROUPS)

    acts_ready(far(1))
    acts_ready(far(2))
    chain(1, True)
    first(1)
    first(2)
    remote(cot_hbm, cot.at[tokens_of(other)], pair_send.at[0], pair_recv.at[0], sibling).wait_recv()

    @pl.loop(3, NZ)
    def _(i):
        acts_ready(far(i))

    def wave(i):
        return lax.rem(z + lax.div(i + 1, 2) * (2 * lax.rem(i, 2) - 1) + NZ, NZ)

    keys[...] = jnp.zeros_like(keys)

    def back_copy(zz, hi):
        return remote(
            back.at[zz, hi], grads.at[:, columns(hi, zz, c)], back_send.at[0], back_recv.at[0], sibling
        )

    def back_arrived(zz, hi):
        return remote(
            back.at[zz, hi], grads.at[:, columns(hi, zz, other)], back_send.at[0], back_recv.at[0], sibling
        )

    def back_of(rows, w):
        product = lax.dot_general(rows, w, (((1,), (1,)), ((), ())), preferred_element_type=F32)
        return (product * out_scale).astype(BF16)

    keys_copy = remote(keys.at[tokens_of(other)], keys_in, pair_send.at[1], pair_recv.at[1], sibling)

    def multiply(zz, last):
        parts = [gathered[zz, :, xx].reshape(block // 2, kw) for xx in range(NX)]
        w = jnp.concatenate(parts, axis=0)
        both = jnp.concatenate([acts[zz, hi] for hi in range(2)], axis=1)
        keys[...] += jnp.dot(both, w, preferred_element_type=F32)

        @pl.when(last)
        def _():
            keys_copy.start()

        for hi in range(2):
            half_w = jnp.concatenate(parts[2 * hi : 2 * hi + 2], axis=0)
            back[zz, hi] = back_of(cot[tokens_of(other), :], half_w)
            back_copy(zz, hi).start()
        for hi in range(2):
            half_w = jnp.concatenate(parts[2 * hi : 2 * hi + 2], axis=0)
            grads[:, columns(hi, zz, c)] = back_of(cot[tokens_of(c), :], half_w)

    def cross_copy(h):
        return remote(
            cross_out.at[h], cross_in.at[h], cross_send.at[0], cross_recv.at[h], along_x[2]
        )

    def chain_end(part):
        for way in range(2):
            for k in (5, 6):
                chain_copy(way, k, part).wait_recv()
        for h in range(2):
            done = share(h, z, x_hi if part else 1 - x_hi)
            done += chain_in[0, 6 - h, part].astype(F32) + chain_in[1, 5 + h, part].astype(F32)
            if part:
                cross_own[h] = done
            else:
                cross_out[h] = done.astype(BF16)
                cross_copy(h).start()

    def outer_results():
        @pl.loop(1, NY)
        def _(d):
            for lo in range(2):
                total_copy(lo * NY + up(y, d, NY), sibling).wait_recv()

        for j in range(GROUPS):
            own = pl.ds(j * piece, piece)
            weights_out[own, :], moved_out[own, :] = nesterov(total[j], master[own, :], momentum[own, :])

    def steps_near(i):
        for j, at in enumerate(NEAR_AT, 1):
            @pl.when(i == at)
            def _():
                zz = wave(j)
                z_arrived(zz).wait_recv()
                if j % 2 == 1 and j < 7:
                    z_copy(zz, 1).start()
                if j % 2 == 0 and j < 6:
                    z_copy(zz, 0).start()
                stage_near(j, zz)

    def steps_line(i):
        @pl.when(jnp.logical_and(i >= LAG_Y + LINE_EARLY, i < NZ + LAG_Y))
        def _():
            stage_line(i - LAG_Y, wave(i - LAG_Y))

    def steps_far(i):
        @pl.when(jnp.logical_and(i >= LAG_F, i < NZ + LAG_F))
        def _():
            stage_far(i - LAG_F, wave(i - LAG_F))

    def steps_last(i):
        @pl.when(i >= LAG_END)
        def _():
            zz = wave(i - LAG_END)
            stage_last(i - LAG_END, zz)
            multiply(zz, i == NZ + LAG_END - 1)

    def steps_first(i):
        @pl.when(i < 6)
        def _():
            first(i + 2)

    def steps_chain(i):
        @pl.when(i < 6)
        def _():
            chain(i + 1, False)

        for part in range(2):
            @pl.when(i == 7 + part)
            def _():
                chain_end(part)

    def steps_row(i):
        @pl.when(i == 1)
        def _():
            first_copy(far(0)).wait_recv()
            line(0, True)

        @pl.when(i == 2)
        def _():
            first_copy(far(1)).wait_recv()
            first_copy(far(2)).wait_recv()
            line(1, True)

        @pl.when(jnp.logical_or(i == 4, i == 6))
        def _():
            first_copy(far(i - 1)).wait_recv()
            first_copy(far(i)).wait_recv()

        @pl.when(jnp.logical_and(i >= 3, i < 8))
        def _():
            line(i - 1, False)

        @pl.when(i == 9)
        def _():
            line_end()

    def steps_total(i):
        @pl.when(i == TOTAL_AT)
        def _():
            total_copy(g, pair_y[0]).start()

        @pl.when(i == TOTAL_ON)
        def _():
            total_copy(pair_g, sibling).wait_recv()
            for d in range(1, NY):
                total_copy(g, along_y[d]).start()
                total_copy(pair_g, along_y[d]).start()

        @pl.when(i == TOTAL_END)
        def _():
            outer_results()

    steps = {
        "near": steps_near, "line": steps_line, "far": steps_far, "last": steps_last,
        "first": steps_first, "chain": steps_chain, "row": steps_row, "total": steps_total,
    }
    if LINE_EARLY:
        stage_line(0, z)

    @pl.loop(1, NZ + LAG_END)
    def _(i):
        for name in ORDER:
            steps[name](i)

    for h in range(2):
        cross_copy(h).wait_recv()
        wgrad_out[pl.ds(h * half, late), :] = (cross_own[h] + cross_in[h].astype(F32)) * out_scale

    keys_copy.wait_recv()
    keys_out[...] = ((keys[tokens_of(c), :] + keys_in[...]) * out_scale).astype(BF16)

    cot_swap.wait_send()
    cot_t_swap.wait_send()
    keys_copy.wait_send()
    for part, sem in (
        (coded.at[pl.ds(0, 7)], coded_send),
        (total.at[pl.ds(0, 7)], total_send),
        (gathered.at[pl.ds(0, 7), 0, 0], z_send),
        (gathered.at[pl.ds(0, 6), 0], x_send),
        (gathered.at[pl.ds(0, 4)], y_send),
        (gathered.at[pl.ds(0, 2)], f_send),
        (chain_out, chain_send),
        (line_out, line_send),
        (first_out, first_send),
        (cross_out, cross_send),
        (back, acts_send),
        (back, back_send),
    ):
        remote(part, part, sem.at[0], pair_recv.at[1], sibling).wait_send()
    remote(back, back, back_send.at[0], back_recv.at[0], sibling).wait_recv()


def finish(weights, moved, keys, grads, turned, weights_hbm, moved_hbm, keys_hbm, grads_hbm, wgrad_hbm, wgrad, sem):
    rows = grads.shape[0] // 4
    pairs = [(grads.at[pl.ds(i * rows, rows)], grads_hbm.at[pl.ds(i * rows, rows)]) for i in range(4)]
    pairs += [(weights, weights_hbm), (moved, moved_hbm), (keys, keys_hbm), (wgrad, wgrad_hbm)]
    copies = [pltpu.make_async_copy(src, dst, sem.at[i]) for i, (src, dst) in enumerate(pairs)]
    for copy in copies[:-1]:
        copy.start()
    wgrad[...] = turned[...].T
    copies[-1].start()
    for copy in copies:
        copy.wait()


def body(delta_codes, master_weights, outer_momentum, activations, key_cotangent):
    tokens, width = activations.shape
    rows, kw = master_weights.shape
    block, piece, half = width // 32, width // 32 // GROUPS, kw // 2
    late = half - CROSS_FIRST
    dma = pltpu.SemaphoreType.DMA
    hbm = pl.BlockSpec(memory_space=pl.ANY)
    vmem = pl.BlockSpec(memory_space=pltpu.VMEM)
    arguments = (delta_codes[0], master_weights, outer_momentum, activations, key_cotangent)
    results = pl.pallas_call(
        kernel,
        name="outer_step",
        out_shape=(
            pltpu.VMEM((rows, kw), F32),
            pltpu.VMEM((rows, kw), F32),
            pltpu.VMEM((tokens, kw), BF16),
            pltpu.VMEM((tokens, width), BF16),
            pltpu.VMEM((kw, block), F32),
        ),
        in_specs=[hbm] * 5,
        out_specs=(vmem,) * 5,
        scratch_shapes=[
            pltpu.VMEM((rows, kw), jnp.int32),
            pltpu.VMEM((rows, kw), F32),
            pltpu.VMEM((rows, kw), F32),
            pltpu.VMEM((2 * tokens, kw), BF16),
            pltpu.VMEM((2, 2, half, tokens), BF16),
            pltpu.VMEM((2, late, 2 * tokens), BF16),
            pltpu.VMEM((2, CROSS_FIRST, 2 * tokens), BF16),
            pltpu.VMEM((NZ, 2, 2 * tokens, block), BF16),
            pltpu.VMEM((GROUPS, piece, kw), BF16),
            pltpu.VMEM((GROUPS, piece, kw), BF16),
            pltpu.VMEM((GROUPS, piece, kw), BF16),
            pltpu.VMEM((NZ, NY, NX, piece, kw), BF16),
            pltpu.VMEM((2, 7, 2, late, block), BF16),
            pltpu.VMEM((2, 7, 2, late, block), BF16),
            pltpu.VMEM((2, late, block), BF16),
            pltpu.VMEM((2, late, block), BF16),
            pltpu.VMEM((2, late, block), F32),
            pltpu.VMEM((NZ, 2, CROSS_FIRST, block), BF16),
            pltpu.VMEM((NZ, 2, CROSS_FIRST, block), BF16),
            pltpu.VMEM((2, 7, CROSS_FIRST, block), BF16),
            pltpu.VMEM((2, 7, CROSS_FIRST, block), BF16),
            pltpu.VMEM((2 * tokens, kw), F32),
            pltpu.VMEM((tokens, kw), F32),
            pltpu.VMEM((NZ, 2, tokens, block), BF16),
            dma((4,)),
            dma((NZ, 2)),
            dma((1,)),
            dma((NZ, 2)),
            dma((3,)),
            dma((3,)),
            dma((1,)),
            dma((GROUPS,)),
            dma((1,)),
            dma((GROUPS,)),
            dma((1,)),
            dma((NZ,)),
            dma((1,)),
            dma((NZ, NX)),
            dma((1,)),
            dma((NZ, 2)),
            dma((1,)),
            dma((NZ, 2)),
            dma((1,)),
            dma((2, 7, 2)),
            dma((1,)),
            dma((2,)),
            dma((1,)),
            dma((NZ,)),
            dma((1,)),
            dma((2, 7)),
            dma((1,)),
            dma((1,)),
        ],
        compiler_params=pltpu.CompilerParams(
            collective_id=0, has_side_effects=True, vmem_limit_bytes=44 * 2**20
        ),
        cost_estimate=pl.CostEstimate(
            flops=6 * tokens * width * kw, bytes_accessed=16 * 2**20, transcendentals=0
        ),
    )(*[pltpu.with_memory_space_constraint(a, pltpu.HBM) for a in arguments])
    weights, moved, keys, grads, wgrad = pl.pallas_call(
        finish,
        name="finish",
        out_shape=(
            jax.ShapeDtypeStruct((rows, kw), F32),
            jax.ShapeDtypeStruct((rows, kw), F32),
            jax.ShapeDtypeStruct((tokens, kw), BF16),
            jax.ShapeDtypeStruct((tokens, width), BF16),
            jax.ShapeDtypeStruct((rows, kw), F32),
        ),
        in_specs=[vmem] * 5,
        out_specs=(hbm,) * 5,
        scratch_shapes=[pltpu.VMEM((rows, kw), F32), dma((8,))],
        compiler_params=pltpu.CompilerParams(vmem_limit_bytes=16 * 2**20),
    )(*[pltpu.with_memory_space_constraint(r, pltpu.VMEM) for r in results])
    return weights, moved, keys, grads, wgrad[None]


def solution(mesh):
    placed = (
        P("group", "fsdp", None),
        P("fsdp", None),
        P("fsdp", None),
        P(("group", "fsdp"), None),
        P(("group", "fsdp"), None),
    )
    return jax.shard_map(
        body,
        mesh=mesh,
        in_specs=placed,
        out_specs=(
            P("fsdp", None),
            P("fsdp", None),
            P(("group", "fsdp"), None),
            P(("group", "fsdp"), None),
            P("group", "fsdp", None),
        ),
        check_vma=False,
    )
```

```python
import functools

import jax
import jax.numpy as jnp
from jax import lax
from jax.experimental import pallas as pl
from jax.experimental.pallas import tpu as pltpu
from jax.sharding import PartitionSpec as P

MESH = pl.DeviceIdType.MESH
F32 = jnp.float32
BF16 = jnp.bfloat16
NX, NY, NZ = 4, 4, 8
GROUPS = 8
LAG_Y, LAG_F, LAG_END = 1, 3, 5
LINE_EARLY = 0
TOTAL_AT, TOTAL_ON, TOTAL_END = 4, 7, 11
NEAR_AT = (1, 1, 2, 2, 3, 3, 6)
ORDER = ("near", "line", "total", "row", "far", "first", "last", "chain")
CROSS_FIRST = 96
TURNED = (4, 6)


def device(x, y, z, c):
    return (lax.rem(x, 2) * 4 + y, lax.div(x, 2) * 16 + z * 2 + c)


def when(condition):
    if isinstance(condition, bool):
        return (lambda f: f()) if condition else (lambda f: None)
    return pl.when(condition)


def quotient(a, b):
    return a // b if isinstance(a, int) else lax.div(a, b)


def remainder(a, b):
    return a % b if isinstance(a, int) else lax.rem(a, b)


def up(v, d, n):
    return lax.rem(v + d, n)


def dequantize(codes):
    values = codes.astype(F32)
    size = jnp.abs(values)
    largest = jnp.max(size, axis=-1, keepdims=True)
    scale = jnp.floor((largest + 0.5) / 127.0) + 1.0
    half = jnp.floor(scale * 0.5)
    magnitude = jnp.floor((size + half + 0.5) / scale)
    signed = jnp.where(values < 0.0, -magnitude, magnitude)
    return signed * scale * (1.0 / 4096.0)


def nesterov(total, weights, momentum):
    outer_grad = total.astype(F32) / GROUPS
    moved = 0.9 * momentum + outer_grad
    return weights - 0.7 * (outer_grad + 0.9 * moved), moved


def kernel(
    delta_hbm, master_hbm, momentum_hbm, acts_hbm, cot_hbm,
    weights_out, moved_out, keys_out, grads, wgrad_out,
    delta, master, momentum, cot, cot_t, late_t, early_t, acts,
    coded, coded_in, total, gathered,
    chain_out, chain_in, cross_out, cross_in, cross_own,
    first_out, first_in, line_out, line_in,
    keys, keys_in, back,
    load_sem, acts_load, acts_send, acts_recv, pair_send, pair_recv,
    coded_send, coded_recv, total_send, total_recv,
    z_send, z_recv, x_send, x_recv, y_send, y_recv, f_send, f_recv,
    chain_send, chain_recv, cross_send, cross_recv,
    first_send, first_recv, line_send, line_recv,
    back_send, back_recv,
):
    tokens, width = acts_hbm.shape
    kw = cot_hbm.shape[1]
    block = width // 32
    piece = block // GROUPS
    half = kw // 2
    late = half - CROSS_FIRST
    out_scale = width ** (-0.5)

    g, f = lax.axis_index("group"), lax.axis_index("fsdp")
    y, x_lo = lax.rem(g, NY), lax.div(g, NY)
    c, z, x_hi = lax.rem(f, 2), lax.rem(lax.div(f, 2), NZ), lax.div(f, 16)
    x = 2 * x_hi + x_lo
    other = 1 - c
    sibling = device(x, y, z, other)
    along_z = [device(x, y, up(z, d, NZ), c) for d in (1, NZ - 1)]
    along_x = [device(up(x, d, NX), y, z, c) for d in range(NX)]
    along_y = [device(x, up(y, d, NY), z, c) for d in range(NY)]
    pair_x = 2 * x_hi + 1 - x_lo
    pair_y = [device(pair_x, up(y, d, NY), z, c) for d in range(NY)]

    def member(j):
        return device(2 * x_hi + lax.div(j, NY), lax.rem(j, NY), z, c)

    def remote(src, dst, send, recv, to):
        return pltpu.make_async_remote_copy(
            src_ref=src, dst_ref=dst, send_sem=send, recv_sem=recv, device_id=to, device_id_type=MESH
        )

    def columns(hi, zz, core):
        return pl.ds(pl.multiple_of((hi * 16 + zz * 2 + core) * block, block), block)

    def tokens_of(core):
        return pl.ds(pl.multiple_of(core * tokens, tokens), tokens)

    def act_load(zz, hi):
        return pltpu.make_async_copy(
            acts_hbm.at[:, columns(hi, zz, c)], acts.at[zz, hi, tokens_of(c)], acts_load.at[zz, hi]
        )

    def act_swap(zz, hi):
        return remote(
            acts_hbm.at[:, columns(hi, zz, other)], acts.at[zz, hi, tokens_of(c)],
            acts_send.at[0], acts_recv.at[zz, hi], sibling,
        )

    def act_arrived(zz, hi):
        return remote(
            acts_hbm.at[:, columns(hi, zz, other)], acts.at[zz, hi, tokens_of(other)],
            acts_send.at[0], acts_recv.at[zz, hi], sibling,
        )

    def far(i):
        step = quotient(i + 1, 2)
        return lax.rem(z + 4 + step * (1 - 2 * remainder(i, 2)) + NZ, NZ)

    loads = [
        pltpu.make_async_copy(delta_hbm, delta, load_sem.at[0]),
        pltpu.make_async_copy(cot_hbm, cot.at[tokens_of(c)], load_sem.at[1]),
        pltpu.make_async_copy(master_hbm, master, load_sem.at[2]),
        pltpu.make_async_copy(momentum_hbm, momentum, load_sem.at[3]),
    ]
    loads[0].start()

    partners = [sibling] + along_z + along_x[1:] + along_y[1:] + pair_y[1:]
    barrier = pltpu.get_barrier_semaphore()
    for partner in partners:
        pl.semaphore_signal(barrier, inc=1, device_id=partner, device_id_type=MESH)
    for load in loads[1:]:
        load.start()
    for hi in range(2):
        act_load(far(0), hi).start()

    loads[0].wait()
    for j in range(GROUPS):
        for k in range(kw // 128):
            codes = delta[pl.ds(j * piece, piece), pl.ds(k * 128, 128)]
            coded[j, :, pl.ds(k * 128, 128)] = dequantize(codes).astype(BF16)
    pl.semaphore_wait(barrier, len(partners))

    def coded_copy(d):
        j = up(g, d, GROUPS)
        return remote(coded.at[j], coded_in.at[g], coded_send.at[0], coded_recv.at[g], member(j))

    def coded_arrived(j):
        return remote(coded.at[j], coded_in.at[j], coded_send.at[0], coded_recv.at[j], sibling)

    @pl.loop(1, GROUPS)
    def _(d):
        coded_copy(d).start()

    for hi in range(2):
        act_swap(far(0), hi).start()
    loads[1].wait()
    cot_t[c] = cot[tokens_of(c), :].T.reshape(2, half, tokens)
    cot_t_swap = remote(cot_t.at[c], cot_t.at[c], pair_send.at[2], pair_recv.at[2], sibling)
    cot_t_swap.start()

    cot_swap = remote(cot_hbm, cot.at[tokens_of(c)], pair_send.at[0], pair_recv.at[0], sibling)
    cot_swap.start()

    @pl.loop(1, NZ)
    def _(i):
        for hi in range(2):
            act_swap(far(i), hi).start()
            act_load(far(i), hi).start()


    def acts_ready(zz):
        for hi in range(2):
            act_load(zz, hi).wait()
            act_arrived(zz, hi).wait_recv()

    def chain_copy(way, k, part):
        return remote(
            chain_out.at[way, k, part], chain_in.at[way, k, part],
            chain_send.at[0], chain_recv.at[way, k, part], along_z[way],
        )

    def share(h, zz, hi):
        return jnp.dot(late_t[h], acts[zz, hi], preferred_element_type=F32)

    def early_share(h, zz, hi):
        return jnp.dot(early_t[h], acts[zz, hi], preferred_element_type=F32)

    def first_copy(zz):
        return remote(
            first_out.at[zz], first_in.at[zz], first_send.at[0], first_recv.at[zz], along_x[2]
        )

    def first(i):
        zz = far(i)
        for h in range(2):
            first_out[zz, h] = early_share(h, zz, 1 - x_hi).astype(BF16)
        first_copy(zz).start()

    def line_copy(way, k):
        return remote(line_out.at[way, k], line_in.at[way, k], line_send.at[0], line_recv.at[way, k], along_z[way])

    def line(k, opening):
        s = quotient(k + 1, 2)
        for way in range(2):
            zz = up(z, 4 - s if way == 0 else 4 + s, NZ)
            h = remainder(k + way, 2)
            if not opening:
                line_copy(way, k - 2).wait_recv()
            sent = early_share(h, zz, x_hi) + first_in[zz, h].astype(F32)
            if not opening:
                sent += line_in[way, k - 2].astype(F32)
            line_out[way, k] = sent.astype(BF16)
            line_copy(way, k).start()

    def line_end():
        first_copy(z).wait_recv()
        for way in range(2):
            for k in (5, 6):
                line_copy(way, k).wait_recv()
        for h in range(2):
            done = early_share(h, z, x_hi) + first_in[z, h].astype(F32)
            done += line_in[0, 6 - h].astype(F32) + line_in[1, 5 + h].astype(F32)
            wgrad_out[pl.ds(h * half + late, CROSS_FIRST), :] = done * out_scale

    def chain(k, opening):
        s = quotient(k + 1, 2)
        for part in range(2):
            for way in range(2):
                zz = up(z, 4 - s if way == 0 else 4 + s, NZ)
                h = remainder(k + way, 2)
                sent = share(h, zz, x_hi if part else 1 - x_hi)
                if not opening:
                    chain_copy(way, k - 2, part).wait_recv()
                    sent += chain_in[way, k - 2, part].astype(F32)
                chain_out[way, k, part] = sent.astype(BF16)
                chain_copy(way, k, part).start()

    remote(cot_t.at[other], cot_t.at[other], pair_send.at[2], pair_recv.at[2], sibling).wait_recv()
    for h in range(2):
        for core in range(2):
            late_t[h, :, pl.ds(core * tokens, tokens)] = cot_t[core, h, :late]
            early_t[h, :, pl.ds(core * tokens, tokens)] = cot_t[core, h, late:]
    acts_ready(far(0))
    chain(0, True)
    first(0)

    rows = pl.ds(pl.multiple_of(g * piece, piece), piece)

    @pl.loop(1, GROUPS)
    def _(d):
        coded_arrived(up(g, d, GROUPS)).wait_recv()

    summed = coded[g].astype(F32)
    for d in range(1, GROUPS):
        summed += coded_in[up(g, d, GROUPS)].astype(F32)
    total[g] = summed.astype(BF16)
    loads[2].wait()
    loads[3].wait()
    updated, _ = nesterov(total[g], master[rows, :], momentum[rows, :])
    gathered[z, y, x] = updated.astype(BF16)

    def z_copy(zz, way):
        return remote(gathered.at[zz, y, x], gathered.at[zz, y, x], z_send.at[0], z_recv.at[zz], along_z[way])

    def z_arrived(zz):
        return remote(gathered.at[zz, y, x], gathered.at[zz, y, x], z_send.at[0], z_recv.at[zz], sibling)

    def near_copy(zz, d, turned):
        to = along_y[d] if turned else along_x[d]
        part = gathered.at[zz, y, x]
        return remote(part, part, x_send.at[0], x_recv.at[zz, y if turned else x], to)

    def near_arrived(zz, d, turned):
        at = up(y if turned else x, d, NX)
        part = gathered.at[zz, at, x] if turned else gathered.at[zz, y, at]
        return remote(part, part, x_send.at[0], x_recv.at[zz, at], sibling)

    def neighbour(way, turned):
        d = 1 if way == 0 else NX - 1
        return along_x[d] if turned else along_y[d]

    def line_of(zz, d, turned):
        return gathered.at[zz, :, up(x, d, NX)] if turned else gathered.at[zz, up(y, d, NY)]

    def half_of(zz, d, way, turned):
        if turned:
            return gathered.at[zz, pl.ds(way * 2, 2), up(x, d, NX)]
        return gathered.at[zz, up(y, d, NY), pl.ds(way * 2, 2)]

    def y_copy(zz, way, turned):
        part = line_of(zz, 0, turned)
        return remote(part, part, y_send.at[0], y_recv.at[zz, way], neighbour(way, turned))

    def y_arrived(zz, way, turned):
        part = line_of(zz, 3 if way == 0 else 1, turned)
        return remote(part, part, y_send.at[0], y_recv.at[zz, way], sibling)

    def f_copy(zz, way, turned):
        part = half_of(zz, 3 if way == 0 else 1, way, turned)
        return remote(part, part, f_send.at[0], f_recv.at[zz, way], neighbour(way, turned))

    def f_arrived(zz, way, turned):
        part = half_of(zz, 2, way, turned)
        return remote(part, part, f_send.at[0], f_recv.at[zz, way], sibling)

    def either(i, step):
        if isinstance(i, int):
            step(i in TURNED)
            return
        hit = i == -1
        for t in TURNED:
            hit = jnp.logical_or(hit, i == t)
        pl.when(hit)(lambda: step(True))
        pl.when(jnp.logical_not(hit))(lambda: step(False))

    def stage_near(i, zz):
        def step(turned):
            for d in range(1, NX):
                near_copy(zz, d, turned).start()

        either(i, step)

    def stage_line(i, zz):
        def step(turned):
            for d in range(1, NX):
                near_arrived(zz, d, turned).wait_recv()
            for way in range(2):
                y_copy(zz, way, turned).start()

        either(i, step)

    def stage_far(i, zz):
        def step(turned):
            for way in range(2):
                y_arrived(zz, way, turned).wait_recv()
            for way in range(2):
                f_copy(zz, way, turned).start()

        either(i, step)

    def stage_last(i, zz):
        def step(turned):
            for way in range(2):
                f_arrived(zz, way, turned).wait_recv()

        either(i, step)

    for way in range(2):
        z_copy(z, way).start()
    stage_near(0, z)

    def total_copy(j, to):
        return remote(total.at[j], total.at[j], total_send.at[0], total_recv.at[j], to)

    pair_g = up(g, NY, GROUPS)

    acts_ready(far(1))
    acts_ready(far(2))
    chain(1, True)
    first(1)
    first(2)
    remote(cot_hbm, cot.at[tokens_of(other)], pair_send.at[0], pair_recv.at[0], sibling).wait_recv()

    @pl.loop(3, NZ)
    def _(i):
        acts_ready(far(i))

    def wave(i):
        return lax.rem(z + quotient(i + 1, 2) * (2 * remainder(i, 2) - 1) + NZ, NZ)

    keys[...] = jnp.zeros_like(keys)

    def back_copy(zz, hi):
        return remote(
            back.at[zz, hi], grads.at[:, columns(hi, zz, c)], back_send.at[0], back_recv.at[0], sibling
        )

    def back_arrived(zz, hi):
        return remote(
            back.at[zz, hi], grads.at[:, columns(hi, zz, other)], back_send.at[0], back_recv.at[0], sibling
        )

    def back_of(rows, w):
        product = lax.dot_general(rows, w, (((1,), (1,)), ((), ())), preferred_element_type=F32)
        return (product * out_scale).astype(BF16)

    keys_copy = remote(keys.at[tokens_of(other)], keys_in, pair_send.at[1], pair_recv.at[1], sibling)

    def multiply(zz, last):
        parts = [gathered[zz, :, xx].reshape(block // 2, kw) for xx in range(NX)]
        w = jnp.concatenate(parts, axis=0)
        both = jnp.concatenate([acts[zz, hi] for hi in range(2)], axis=1)
        keys[...] += jnp.dot(both, w, preferred_element_type=F32)

        @when(last)
        def _():
            keys_copy.start()

        for hi in range(2):
            half_w = jnp.concatenate(parts[2 * hi : 2 * hi + 2], axis=0)
            back[zz, hi] = back_of(cot[tokens_of(other), :], half_w)
            back_copy(zz, hi).start()
        for hi in range(2):
            half_w = jnp.concatenate(parts[2 * hi : 2 * hi + 2], axis=0)
            grads[:, columns(hi, zz, c)] = back_of(cot[tokens_of(c), :], half_w)

    def cross_copy(h):
        return remote(
            cross_out.at[h], cross_in.at[h], cross_send.at[0], cross_recv.at[h], along_x[2]
        )

    def chain_end(part):
        for way in range(2):
            for k in (5, 6):
                chain_copy(way, k, part).wait_recv()
        for h in range(2):
            done = share(h, z, x_hi if part else 1 - x_hi)
            done += chain_in[0, 6 - h, part].astype(F32) + chain_in[1, 5 + h, part].astype(F32)
            if part:
                cross_own[h] = done
            else:
                cross_out[h] = done.astype(BF16)
                cross_copy(h).start()

    def outer_results():
        @pl.loop(1, NY)
        def _(d):
            for lo in range(2):
                total_copy(lo * NY + up(y, d, NY), sibling).wait_recv()

        for j in range(GROUPS):
            own = pl.ds(j * piece, piece)
            weights_out[own, :], moved_out[own, :] = nesterov(total[j], master[own, :], momentum[own, :])

    def steps_near(i):
        for j, at in enumerate(NEAR_AT, 1):
            @when(i == at)
            def _():
                zz = wave(j)
                z_arrived(zz).wait_recv()
                if j % 2 == 1 and j < 7:
                    z_copy(zz, 1).start()
                if j % 2 == 0 and j < 6:
                    z_copy(zz, 0).start()
                stage_near(j, zz)

    def steps_line(i):
        @when(i >= LAG_Y + LINE_EARLY and i < NZ + LAG_Y)
        def _():
            stage_line(i - LAG_Y, wave(i - LAG_Y))

    def steps_far(i):
        @when(i >= LAG_F and i < NZ + LAG_F)
        def _():
            stage_far(i - LAG_F, wave(i - LAG_F))

    def steps_last(i):
        @when(i >= LAG_END)
        def _():
            zz = wave(i - LAG_END)
            stage_last(i - LAG_END, zz)
            multiply(zz, i == NZ + LAG_END - 1)

    def steps_first(i):
        @when(i < 6)
        def _():
            first(i + 2)

    def steps_chain(i):
        @when(i < 6)
        def _():
            chain(i + 1, False)

        for part in range(2):
            @when(i == 7 + part)
            def _():
                chain_end(part)

    def steps_row(i):
        @when(i == 1)
        def _():
            first_copy(far(0)).wait_recv()
            line(0, True)

        @when(i == 2)
        def _():
            first_copy(far(1)).wait_recv()
            first_copy(far(2)).wait_recv()
            line(1, True)

        @when(i == 4 or i == 6)
        def _():
            first_copy(far(i - 1)).wait_recv()
            first_copy(far(i)).wait_recv()

        @when(i >= 3 and i < 8)
        def _():
            line(i - 1, False)

        @when(i == 9)
        def _():
            line_end()

    def steps_total(i):
        @when(i == TOTAL_AT)
        def _():
            total_copy(g, pair_y[0]).start()

        @when(i == TOTAL_ON)
        def _():
            total_copy(pair_g, sibling).wait_recv()
            for d in range(1, NY):
                total_copy(g, along_y[d]).start()
                total_copy(pair_g, along_y[d]).start()

        @when(i == TOTAL_END)
        def _():
            outer_results()

    steps = {
        "near": steps_near, "line": steps_line, "far": steps_far, "last": steps_last,
        "first": steps_first, "chain": steps_chain, "row": steps_row, "total": steps_total,
    }
    if LINE_EARLY:
        stage_line(0, z)

    for i in range(1, NZ + LAG_END):
        for name in ORDER:
            steps[name](i)

    for h in range(2):
        cross_copy(h).wait_recv()
        wgrad_out[pl.ds(h * half, late), :] = (cross_own[h] + cross_in[h].astype(F32)) * out_scale

    keys_copy.wait_recv()
    keys_out[...] = ((keys[tokens_of(c), :] + keys_in[...]) * out_scale).astype(BF16)

    cot_swap.wait_send()
    cot_t_swap.wait_send()
    keys_copy.wait_send()
    for part, sem in (
        (coded.at[pl.ds(0, 7)], coded_send),
        (total.at[pl.ds(0, 7)], total_send),
        (gathered.at[pl.ds(0, 7), 0, 0], z_send),
        (gathered.at[pl.ds(0, 6), 0], x_send),
        (gathered.at[pl.ds(0, 4)], y_send),
        (gathered.at[pl.ds(0, 2)], f_send),
        (chain_out, chain_send),
        (line_out, line_send),
        (first_out, first_send),
        (cross_out, cross_send),
        (back, acts_send),
        (back, back_send),
    ):
        remote(part, part, sem.at[0], pair_recv.at[1], sibling).wait_send()
    remote(back, back, back_send.at[0], back_recv.at[0], sibling).wait_recv()


def finish(weights, moved, keys, grads, turned, weights_hbm, moved_hbm, keys_hbm, grads_hbm, wgrad_hbm, wgrad, sem):
    rows = grads.shape[0] // 4
    pairs = [(grads.at[pl.ds(i * rows, rows)], grads_hbm.at[pl.ds(i * rows, rows)]) for i in range(4)]
    pairs += [(weights, weights_hbm), (moved, moved_hbm), (keys, keys_hbm), (wgrad, wgrad_hbm)]
    copies = [pltpu.make_async_copy(src, dst, sem.at[i]) for i, (src, dst) in enumerate(pairs)]
    for copy in copies[:-1]:
        copy.start()
    wgrad[...] = turned[...].T
    copies[-1].start()
    for copy in copies:
        copy.wait()


def body(delta_codes, master_weights, outer_momentum, activations, key_cotangent):
    tokens, width = activations.shape
    rows, kw = master_weights.shape
    block, piece, half = width // 32, width // 32 // GROUPS, kw // 2
    late = half - CROSS_FIRST
    dma = pltpu.SemaphoreType.DMA
    hbm = pl.BlockSpec(memory_space=pl.ANY)
    vmem = pl.BlockSpec(memory_space=pltpu.VMEM)
    arguments = (delta_codes[0], master_weights, outer_momentum, activations, key_cotangent)
    results = pl.pallas_call(
        kernel,
        name="outer_step",
        out_shape=(
            pltpu.VMEM((rows, kw), F32),
            pltpu.VMEM((rows, kw), F32),
            pltpu.VMEM((tokens, kw), BF16),
            pltpu.VMEM((tokens, width), BF16),
            pltpu.VMEM((kw, block), F32),
        ),
        in_specs=[hbm] * 5,
        out_specs=(vmem,) * 5,
        scratch_shapes=[
            pltpu.VMEM((rows, kw), jnp.int32),
            pltpu.VMEM((rows, kw), F32),
            pltpu.VMEM((rows, kw), F32),
            pltpu.VMEM((2 * tokens, kw), BF16),
            pltpu.VMEM((2, 2, half, tokens), BF16),
            pltpu.VMEM((2, late, 2 * tokens), BF16),
            pltpu.VMEM((2, CROSS_FIRST, 2 * tokens), BF16),
            pltpu.VMEM((NZ, 2, 2 * tokens, block), BF16),
            pltpu.VMEM((GROUPS, piece, kw), BF16),
            pltpu.VMEM((GROUPS, piece, kw), BF16),
            pltpu.VMEM((GROUPS, piece, kw), BF16),
            pltpu.VMEM((NZ, NY, NX, piece, kw), BF16),
            pltpu.VMEM((2, 7, 2, late, block), BF16),
            pltpu.VMEM((2, 7, 2, late, block), BF16),
            pltpu.VMEM((2, late, block), BF16),
            pltpu.VMEM((2, late, block), BF16),
            pltpu.VMEM((2, late, block), F32),
            pltpu.VMEM((NZ, 2, CROSS_FIRST, block), BF16),
            pltpu.VMEM((NZ, 2, CROSS_FIRST, block), BF16),
            pltpu.VMEM((2, 7, CROSS_FIRST, block), BF16),
            pltpu.VMEM((2, 7, CROSS_FIRST, block), BF16),
            pltpu.VMEM((2 * tokens, kw), F32),
            pltpu.VMEM((tokens, kw), F32),
            pltpu.VMEM((NZ, 2, tokens, block), BF16),
            dma((4,)),
            dma((NZ, 2)),
            dma((1,)),
            dma((NZ, 2)),
            dma((3,)),
            dma((3,)),
            dma((1,)),
            dma((GROUPS,)),
            dma((1,)),
            dma((GROUPS,)),
            dma((1,)),
            dma((NZ,)),
            dma((1,)),
            dma((NZ, NX)),
            dma((1,)),
            dma((NZ, 2)),
            dma((1,)),
            dma((NZ, 2)),
            dma((1,)),
            dma((2, 7, 2)),
            dma((1,)),
            dma((2,)),
            dma((1,)),
            dma((NZ,)),
            dma((1,)),
            dma((2, 7)),
            dma((1,)),
            dma((1,)),
        ],
        compiler_params=pltpu.CompilerParams(
            collective_id=0, has_side_effects=True, vmem_limit_bytes=44 * 2**20
        ),
        cost_estimate=pl.CostEstimate(
            flops=6 * tokens * width * kw, bytes_accessed=16 * 2**20, transcendentals=0
        ),
    )(*[pltpu.with_memory_space_constraint(a, pltpu.HBM) for a in arguments])
    weights, moved, keys, grads, wgrad = pl.pallas_call(
        finish,
        name="finish",
        out_shape=(
            jax.ShapeDtypeStruct((rows, kw), F32),
            jax.ShapeDtypeStruct((rows, kw), F32),
            jax.ShapeDtypeStruct((tokens, kw), BF16),
            jax.ShapeDtypeStruct((tokens, width), BF16),
            jax.ShapeDtypeStruct((rows, kw), F32),
        ),
        in_specs=[vmem] * 5,
        out_specs=(hbm,) * 5,
        scratch_shapes=[pltpu.VMEM((rows, kw), F32), dma((8,))],
        compiler_params=pltpu.CompilerParams(vmem_limit_bytes=16 * 2**20),
    )(*[pltpu.with_memory_space_constraint(r, pltpu.VMEM) for r in results])
    return weights, moved, keys, grads, wgrad[None]


def solution(mesh):
    placed = (
        P("group", "fsdp", None),
        P("fsdp", None),
        P("fsdp", None),
        P(("group", "fsdp"), None),
        P(("group", "fsdp"), None),
    )
    return jax.shard_map(
        body,
        mesh=mesh,
        in_specs=placed,
        out_specs=(
            P("fsdp", None),
            P("fsdp", None),
            P(("group", "fsdp"), None),
            P(("group", "fsdp"), None),
            P("group", "fsdp", None),
        ),
        check_vma=False,
    )
```

```python
import functools

import jax
import jax.numpy as jnp
from jax import lax
from jax.experimental import pallas as pl
from jax.experimental.pallas import tpu as pltpu
from jax.sharding import PartitionSpec as P

MESH = pl.DeviceIdType.MESH
F32 = jnp.float32
BF16 = jnp.bfloat16
NX, NY, NZ = 4, 4, 8
GROUPS = 8
LAG_Y, LAG_F, LAG_END = 1, 3, 5
LINE_EARLY = 1
TOTAL_AT, TOTAL_ON, TOTAL_END = 4, 7, 11
NEAR_AT = (1, 1, 2, 2, 3, 3, 6)
ORDER = ("near", "line", "total", "row", "far", "first", "last", "chain")
CROSS_FIRST = 96
TURNED = (4, 6)


def device(x, y, z, c):
    return (lax.rem(x, 2) * 4 + y, lax.div(x, 2) * 16 + z * 2 + c)


def when(condition):
    if isinstance(condition, bool):
        return (lambda f: f()) if condition else (lambda f: None)
    return pl.when(condition)


def quotient(a, b):
    return a // b if isinstance(a, int) else lax.div(a, b)


def remainder(a, b):
    return a % b if isinstance(a, int) else lax.rem(a, b)


def up(v, d, n):
    return lax.rem(v + d, n)


def dequantize(codes):
    values = codes.astype(F32)
    size = jnp.abs(values)
    largest = jnp.max(size, axis=-1, keepdims=True)
    scale = jnp.floor((largest + 0.5) / 127.0) + 1.0
    half = jnp.floor(scale * 0.5)
    magnitude = jnp.floor((size + half + 0.5) / scale)
    signed = jnp.where(values < 0.0, -magnitude, magnitude)
    return signed * scale * (1.0 / 4096.0)


def nesterov(total, weights, momentum):
    outer_grad = total.astype(F32) / GROUPS
    moved = 0.9 * momentum + outer_grad
    return weights - 0.7 * (outer_grad + 0.9 * moved), moved


def kernel(
    delta_hbm, master_hbm, momentum_hbm, acts_hbm, cot_hbm,
    weights_out, moved_out, keys_out, grads, wgrad_out,
    delta, master, momentum, cot, cot_t, late_t, early_t, acts,
    coded, coded_in, total, gathered,
    chain_out, chain_in, cross_out, cross_in, cross_own,
    first_out, first_in, line_out, line_in,
    keys, keys_in, back,
    load_sem, acts_load, acts_send, acts_recv, pair_send, pair_recv,
    coded_send, coded_recv, total_send, total_recv,
    z_send, z_recv, x_send, x_recv, y_send, y_recv, f_send, f_recv,
    chain_send, chain_recv, cross_send, cross_recv,
    first_send, first_recv, line_send, line_recv,
    back_send, back_recv,
):
    tokens, width = acts_hbm.shape
    kw = cot_hbm.shape[1]
    block = width // 32
    piece = block // GROUPS
    half = kw // 2
    late = half - CROSS_FIRST
    out_scale = width ** (-0.5)

    g, f = lax.axis_index("group"), lax.axis_index("fsdp")
    y, x_lo = lax.rem(g, NY), lax.div(g, NY)
    c, z, x_hi = lax.rem(f, 2), lax.rem(lax.div(f, 2), NZ), lax.div(f, 16)
    x = 2 * x_hi + x_lo
    other = 1 - c
    sibling = device(x, y, z, other)
    along_z = [device(x, y, up(z, d, NZ), c) for d in (1, NZ - 1)]
    along_x = [device(up(x, d, NX), y, z, c) for d in range(NX)]
    along_y = [device(x, up(y, d, NY), z, c) for d in range(NY)]
    pair_x = 2 * x_hi + 1 - x_lo
    pair_y = [device(pair_x, up(y, d, NY), z, c) for d in range(NY)]

    def member(j):
        return device(2 * x_hi + lax.div(j, NY), lax.rem(j, NY), z, c)

    def remote(src, dst, send, recv, to):
        return pltpu.make_async_remote_copy(
            src_ref=src, dst_ref=dst, send_sem=send, recv_sem=recv, device_id=to, device_id_type=MESH
        )

    def columns(hi, zz, core):
        return pl.ds(pl.multiple_of((hi * 16 + zz * 2 + core) * block, block), block)

    def tokens_of(core):
        return pl.ds(pl.multiple_of(core * tokens, tokens), tokens)

    def act_load(zz, hi):
        return pltpu.make_async_copy(
            acts_hbm.at[:, columns(hi, zz, c)], acts.at[zz, hi, tokens_of(c)], acts_load.at[zz, hi]
        )

    def act_swap(zz, hi):
        return remote(
            acts_hbm.at[:, columns(hi, zz, other)], acts.at[zz, hi, tokens_of(c)],
            acts_send.at[0], acts_recv.at[zz, hi], sibling,
        )

    def act_arrived(zz, hi):
        return remote(
            acts_hbm.at[:, columns(hi, zz, other)], acts.at[zz, hi, tokens_of(other)],
            acts_send.at[0], acts_recv.at[zz, hi], sibling,
        )

    def far(i):
        step = quotient(i + 1, 2)
        return lax.rem(z + 4 + step * (1 - 2 * remainder(i, 2)) + NZ, NZ)

    loads = [
        pltpu.make_async_copy(delta_hbm, delta, load_sem.at[0]),
        pltpu.make_async_copy(cot_hbm, cot.at[tokens_of(c)], load_sem.at[1]),
        pltpu.make_async_copy(master_hbm, master, load_sem.at[2]),
        pltpu.make_async_copy(momentum_hbm, momentum, load_sem.at[3]),
    ]
    loads[0].start()

    partners = [sibling] + along_z + along_x[1:] + along_y[1:] + pair_y[1:]
    barrier = pltpu.get_barrier_semaphore()
    for partner in partners:
        pl.semaphore_signal(barrier, inc=1, device_id=partner, device_id_type=MESH)
    for load in loads[1:]:
        load.start()
    for hi in range(2):
        act_load(far(0), hi).start()

    loads[0].wait()
    for j in range(GROUPS):
        for k in range(kw // 128):
            codes = delta[pl.ds(j * piece, piece), pl.ds(k * 128, 128)]
            coded[j, :, pl.ds(k * 128, 128)] = dequantize(codes).astype(BF16)
    pl.semaphore_wait(barrier, len(partners))

    def coded_copy(d):
        j = up(g, d, GROUPS)
        return remote(coded.at[j], coded_in.at[g], coded_send.at[0], coded_recv.at[g], member(j))

    def coded_arrived(j):
        return remote(coded.at[j], coded_in.at[j], coded_send.at[0], coded_recv.at[j], sibling)

    @pl.loop(1, GROUPS)
    def _(d):
        coded_copy(d).start()

    for hi in range(2):
        act_swap(far(0), hi).start()
    loads[1].wait()
    cot_t[c] = cot[tokens_of(c), :].T.reshape(2, half, tokens)
    cot_t_swap = remote(cot_t.at[c], cot_t.at[c], pair_send.at[2], pair_recv.at[2], sibling)
    cot_t_swap.start()

    cot_swap = remote(cot_hbm, cot.at[tokens_of(c)], pair_send.at[0], pair_recv.at[0], sibling)
    cot_swap.start()

    @pl.loop(1, NZ)
    def _(i):
        for hi in range(2):
            act_swap(far(i), hi).start()
            act_load(far(i), hi).start()


    def acts_ready(zz):
        for hi in range(2):
            act_load(zz, hi).wait()
            act_arrived(zz, hi).wait_recv()

    def chain_copy(way, k, part):
        return remote(
            chain_out.at[way, k, part], chain_in.at[way, k, part],
            chain_send.at[0], chain_recv.at[way, k, part], along_z[way],
        )

    def share(h, zz, hi):
        return jnp.dot(late_t[h], acts[zz, hi], preferred_element_type=F32)

    def early_share(h, zz, hi):
        return jnp.dot(early_t[h], acts[zz, hi], preferred_element_type=F32)

    def first_copy(zz):
        return remote(
            first_out.at[zz], first_in.at[zz], first_send.at[0], first_recv.at[zz], along_x[2]
        )

    def first(i):
        zz = far(i)
        for h in range(2):
            first_out[zz, h] = early_share(h, zz, 1 - x_hi).astype(BF16)
        first_copy(zz).start()

    def line_copy(way, k):
        return remote(line_out.at[way, k], line_in.at[way, k], line_send.at[0], line_recv.at[way, k], along_z[way])

    def line(k, opening):
        s = quotient(k + 1, 2)
        for way in range(2):
            zz = up(z, 4 - s if way == 0 else 4 + s, NZ)
            h = remainder(k + way, 2)
            if not opening:
                line_copy(way, k - 2).wait_recv()
            sent = early_share(h, zz, x_hi) + first_in[zz, h].astype(F32)
            if not opening:
                sent += line_in[way, k - 2].astype(F32)
            line_out[way, k] = sent.astype(BF16)
            line_copy(way, k).start()

    def line_end():
        first_copy(z).wait_recv()
        for way in range(2):
            for k in (5, 6):
                line_copy(way, k).wait_recv()
        for h in range(2):
            done = early_share(h, z, x_hi) + first_in[z, h].astype(F32)
            done += line_in[0, 6 - h].astype(F32) + line_in[1, 5 + h].astype(F32)
            wgrad_out[pl.ds(h * half + late, CROSS_FIRST), :] = done * out_scale

    def chain(k, opening):
        s = quotient(k + 1, 2)
        for part in range(2):
            for way in range(2):
                zz = up(z, 4 - s if way == 0 else 4 + s, NZ)
                h = remainder(k + way, 2)
                sent = share(h, zz, x_hi if part else 1 - x_hi)
                if not opening:
                    chain_copy(way, k - 2, part).wait_recv()
                    sent += chain_in[way, k - 2, part].astype(F32)
                chain_out[way, k, part] = sent.astype(BF16)
                chain_copy(way, k, part).start()

    remote(cot_t.at[other], cot_t.at[other], pair_send.at[2], pair_recv.at[2], sibling).wait_recv()
    for h in range(2):
        for core in range(2):
            late_t[h, :, pl.ds(core * tokens, tokens)] = cot_t[core, h, :late]
            early_t[h, :, pl.ds(core * tokens, tokens)] = cot_t[core, h, late:]
    acts_ready(far(0))
    chain(0, True)
    first(0)
    acts_ready(far(1))
    first(1)

    rows = pl.ds(pl.multiple_of(g * piece, piece), piece)

    @pl.loop(1, GROUPS)
    def _(d):
        coded_arrived(up(g, d, GROUPS)).wait_recv()

    summed = coded[g].astype(F32)
    for d in range(1, GROUPS):
        summed += coded_in[up(g, d, GROUPS)].astype(F32)
    total[g] = summed.astype(BF16)
    loads[2].wait()
    loads[3].wait()
    updated, _ = nesterov(total[g], master[rows, :], momentum[rows, :])
    gathered[z, y, x] = updated.astype(BF16)

    def z_copy(zz, way):
        return remote(gathered.at[zz, y, x], gathered.at[zz, y, x], z_send.at[0], z_recv.at[zz], along_z[way])

    def z_arrived(zz):
        return remote(gathered.at[zz, y, x], gathered.at[zz, y, x], z_send.at[0], z_recv.at[zz], sibling)

    def near_copy(zz, d, turned):
        to = along_y[d] if turned else along_x[d]
        part = gathered.at[zz, y, x]
        return remote(part, part, x_send.at[0], x_recv.at[zz, y if turned else x], to)

    def near_arrived(zz, d, turned):
        at = up(y if turned else x, d, NX)
        part = gathered.at[zz, at, x] if turned else gathered.at[zz, y, at]
        return remote(part, part, x_send.at[0], x_recv.at[zz, at], sibling)

    def neighbour(way, turned):
        d = 1 if way == 0 else NX - 1
        return along_x[d] if turned else along_y[d]

    def line_of(zz, d, turned):
        return gathered.at[zz, :, up(x, d, NX)] if turned else gathered.at[zz, up(y, d, NY)]

    def half_of(zz, d, way, turned):
        if turned:
            return gathered.at[zz, pl.ds(way * 2, 2), up(x, d, NX)]
        return gathered.at[zz, up(y, d, NY), pl.ds(way * 2, 2)]

    def y_copy(zz, way, turned):
        part = line_of(zz, 0, turned)
        return remote(part, part, y_send.at[0], y_recv.at[zz, way], neighbour(way, turned))

    def y_arrived(zz, way, turned):
        part = line_of(zz, 3 if way == 0 else 1, turned)
        return remote(part, part, y_send.at[0], y_recv.at[zz, way], sibling)

    def f_copy(zz, way, turned):
        part = half_of(zz, 3 if way == 0 else 1, way, turned)
        return remote(part, part, f_send.at[0], f_recv.at[zz, way], neighbour(way, turned))

    def f_arrived(zz, way, turned):
        part = half_of(zz, 2, way, turned)
        return remote(part, part, f_send.at[0], f_recv.at[zz, way], sibling)

    def either(i, step):
        if isinstance(i, int):
            step(i in TURNED)
            return
        hit = i == -1
        for t in TURNED:
            hit = jnp.logical_or(hit, i == t)
        pl.when(hit)(lambda: step(True))
        pl.when(jnp.logical_not(hit))(lambda: step(False))

    def stage_near(i, zz):
        def step(turned):
            for d in range(1, NX):
                near_copy(zz, d, turned).start()

        either(i, step)

    def stage_line(i, zz):
        def step(turned):
            for d in range(1, NX):
                near_arrived(zz, d, turned).wait_recv()
            for way in range(2):
                y_copy(zz, way, turned).start()

        either(i, step)

    def stage_far(i, zz):
        def step(turned):
            for way in range(2):
                y_arrived(zz, way, turned).wait_recv()
            for way in range(2):
                f_copy(zz, way, turned).start()

        either(i, step)

    def stage_last(i, zz):
        def step(turned):
            for way in range(2):
                f_arrived(zz, way, turned).wait_recv()

        either(i, step)

    for way in range(2):
        z_copy(z, way).start()
    stage_near(0, z)

    def total_copy(j, to):
        return remote(total.at[j], total.at[j], total_send.at[0], total_recv.at[j], to)

    pair_g = up(g, NY, GROUPS)

    acts_ready(far(2))
    chain(1, True)
    first(2)
    remote(cot_hbm, cot.at[tokens_of(other)], pair_send.at[0], pair_recv.at[0], sibling).wait_recv()

    @pl.loop(3, NZ)
    def _(i):
        acts_ready(far(i))

    def wave(i):
        return lax.rem(z + quotient(i + 1, 2) * (2 * remainder(i, 2) - 1) + NZ, NZ)

    keys[...] = jnp.zeros_like(keys)

    def back_copy(zz, hi):
        return remote(
            back.at[zz, hi], grads.at[:, columns(hi, zz, c)], back_send.at[0], back_recv.at[0], sibling
        )

    def back_arrived(zz, hi):
        return remote(
            back.at[zz, hi], grads.at[:, columns(hi, zz, other)], back_send.at[0], back_recv.at[0], sibling
        )

    def back_of(rows, w):
        product = lax.dot_general(rows, w, (((1,), (1,)), ((), ())), preferred_element_type=F32)
        return (product * out_scale).astype(BF16)

    keys_copy = remote(keys.at[tokens_of(other)], keys_in, pair_send.at[1], pair_recv.at[1], sibling)

    def multiply(zz, last):
        parts = [gathered[zz, :, xx].reshape(block // 2, kw) for xx in range(NX)]
        w = jnp.concatenate(parts, axis=0)
        both = jnp.concatenate([acts[zz, hi] for hi in range(2)], axis=1)
        keys[...] += jnp.dot(both, w, preferred_element_type=F32)

        @when(last)
        def _():
            keys_copy.start()

        for hi in range(2):
            half_w = jnp.concatenate(parts[2 * hi : 2 * hi + 2], axis=0)
            back[zz, hi] = back_of(cot[tokens_of(other), :], half_w)
            back_copy(zz, hi).start()
        for hi in range(2):
            half_w = jnp.concatenate(parts[2 * hi : 2 * hi + 2], axis=0)
            grads[:, columns(hi, zz, c)] = back_of(cot[tokens_of(c), :], half_w)

    def cross_copy(h):
        return remote(
            cross_out.at[h], cross_in.at[h], cross_send.at[0], cross_recv.at[h], along_x[2]
        )

    def chain_end(part):
        for way in range(2):
            for k in (5, 6):
                chain_copy(way, k, part).wait_recv()
        for h in range(2):
            done = share(h, z, x_hi if part else 1 - x_hi)
            done += chain_in[0, 6 - h, part].astype(F32) + chain_in[1, 5 + h, part].astype(F32)
            if part:
                cross_own[h] = done
            else:
                cross_out[h] = done.astype(BF16)
                cross_copy(h).start()

    def outer_results():
        @pl.loop(1, NY)
        def _(d):
            for lo in range(2):
                total_copy(lo * NY + up(y, d, NY), sibling).wait_recv()

        for j in range(GROUPS):
            own = pl.ds(j * piece, piece)
            weights_out[own, :], moved_out[own, :] = nesterov(total[j], master[own, :], momentum[own, :])

    def steps_near(i):
        for j, at in enumerate(NEAR_AT, 1):
            @when(i == at)
            def _():
                zz = wave(j)
                z_arrived(zz).wait_recv()
                if j % 2 == 1 and j < 7:
                    z_copy(zz, 1).start()
                if j % 2 == 0 and j < 6:
                    z_copy(zz, 0).start()
                stage_near(j, zz)

    def steps_line(i):
        @when(i >= LAG_Y + LINE_EARLY and i < NZ + LAG_Y)
        def _():
            stage_line(i - LAG_Y, wave(i - LAG_Y))

    def steps_far(i):
        @when(i >= LAG_F and i < NZ + LAG_F)
        def _():
            stage_far(i - LAG_F, wave(i - LAG_F))

    def steps_last(i):
        @when(i >= LAG_END)
        def _():
            zz = wave(i - LAG_END)
            stage_last(i - LAG_END, zz)
            multiply(zz, i == NZ + LAG_END - 1)

    def steps_first(i):
        @when(i < 6)
        def _():
            first(i + 2)

    def steps_chain(i):
        @when(i < 6)
        def _():
            chain(i + 1, False)

        for part in range(2):
            @when(i == 7 + part)
            def _():
                chain_end(part)

    def steps_row(i):
        @when(i == 1)
        def _():
            first_copy(far(0)).wait_recv()
            line(0, True)

        @when(i == 2)
        def _():
            first_copy(far(1)).wait_recv()
            first_copy(far(2)).wait_recv()
            line(1, True)

        @when(i == 4 or i == 6)
        def _():
            first_copy(far(i - 1)).wait_recv()
            first_copy(far(i)).wait_recv()

        @when(i >= 3 and i < 8)
        def _():
            line(i - 1, False)

        @when(i == 9)
        def _():
            line_end()

    def steps_total(i):
        @when(i == TOTAL_AT)
        def _():
            total_copy(g, pair_y[0]).start()

        @when(i == TOTAL_ON)
        def _():
            total_copy(pair_g, sibling).wait_recv()
            for d in range(1, NY):
                total_copy(g, along_y[d]).start()
                total_copy(pair_g, along_y[d]).start()

        @when(i == TOTAL_END)
        def _():
            outer_results()

    steps = {
        "near": steps_near, "line": steps_line, "far": steps_far, "last": steps_last,
        "first": steps_first, "chain": steps_chain, "row": steps_row, "total": steps_total,
    }
    if LINE_EARLY:
        stage_line(0, z)

    for i in range(1, NZ + LAG_END):
        for name in ORDER:
            steps[name](i)

    for h in range(2):
        cross_copy(h).wait_recv()
        wgrad_out[pl.ds(h * half, late), :] = (cross_own[h] + cross_in[h].astype(F32)) * out_scale

    keys_copy.wait_recv()
    keys_out[...] = ((keys[tokens_of(c), :] + keys_in[...]) * out_scale).astype(BF16)

    cot_swap.wait_send()
    cot_t_swap.wait_send()
    keys_copy.wait_send()
    for part, sem in (
        (coded.at[pl.ds(0, 7)], coded_send),
        (total.at[pl.ds(0, 7)], total_send),
        (gathered.at[pl.ds(0, 7), 0, 0], z_send),
        (gathered.at[pl.ds(0, 6), 0], x_send),
        (gathered.at[pl.ds(0, 4)], y_send),
        (gathered.at[pl.ds(0, 2)], f_send),
        (chain_out, chain_send),
        (line_out, line_send),
        (first_out, first_send),
        (cross_out, cross_send),
        (back, acts_send),
        (back, back_send),
    ):
        remote(part, part, sem.at[0], pair_recv.at[1], sibling).wait_send()
    remote(back, back, back_send.at[0], back_recv.at[0], sibling).wait_recv()


def finish(weights, moved, keys, grads, turned, weights_hbm, moved_hbm, keys_hbm, grads_hbm, wgrad_hbm, wgrad, sem):
    rows = grads.shape[0] // 4
    pairs = [(grads.at[pl.ds(i * rows, rows)], grads_hbm.at[pl.ds(i * rows, rows)]) for i in range(4)]
    pairs += [(weights, weights_hbm), (moved, moved_hbm), (keys, keys_hbm), (wgrad, wgrad_hbm)]
    copies = [pltpu.make_async_copy(src, dst, sem.at[i]) for i, (src, dst) in enumerate(pairs)]
    for copy in copies[:-1]:
        copy.start()
    wgrad[...] = turned[...].T
    copies[-1].start()
    for copy in copies:
        copy.wait()


def body(delta_codes, master_weights, outer_momentum, activations, key_cotangent):
    tokens, width = activations.shape
    rows, kw = master_weights.shape
    block, piece, half = width // 32, width // 32 // GROUPS, kw // 2
    late = half - CROSS_FIRST
    dma = pltpu.SemaphoreType.DMA
    hbm = pl.BlockSpec(memory_space=pl.ANY)
    vmem = pl.BlockSpec(memory_space=pltpu.VMEM)
    arguments = (delta_codes[0], master_weights, outer_momentum, activations, key_cotangent)
    results = pl.pallas_call(
        kernel,
        name="outer_step",
        out_shape=(
            pltpu.VMEM((rows, kw), F32),
            pltpu.VMEM((rows, kw), F32),
            pltpu.VMEM((tokens, kw), BF16),
            pltpu.VMEM((tokens, width), BF16),
            pltpu.VMEM((kw, block), F32),
        ),
        in_specs=[hbm] * 5,
        out_specs=(vmem,) * 5,
        scratch_shapes=[
            pltpu.VMEM((rows, kw), jnp.int32),
            pltpu.VMEM((rows, kw), F32),
            pltpu.VMEM((rows, kw), F32),
            pltpu.VMEM((2 * tokens, kw), BF16),
            pltpu.VMEM((2, 2, half, tokens), BF16),
            pltpu.VMEM((2, late, 2 * tokens), BF16),
            pltpu.VMEM((2, CROSS_FIRST, 2 * tokens), BF16),
            pltpu.VMEM((NZ, 2, 2 * tokens, block), BF16),
            pltpu.VMEM((GROUPS, piece, kw), BF16),
            pltpu.VMEM((GROUPS, piece, kw), BF16),
            pltpu.VMEM((GROUPS, piece, kw), BF16),
            pltpu.VMEM((NZ, NY, NX, piece, kw), BF16),
            pltpu.VMEM((2, 7, 2, late, block), BF16),
            pltpu.VMEM((2, 7, 2, late, block), BF16),
            pltpu.VMEM((2, late, block), BF16),
            pltpu.VMEM((2, late, block), BF16),
            pltpu.VMEM((2, late, block), F32),
            pltpu.VMEM((NZ, 2, CROSS_FIRST, block), BF16),
            pltpu.VMEM((NZ, 2, CROSS_FIRST, block), BF16),
            pltpu.VMEM((2, 7, CROSS_FIRST, block), BF16),
            pltpu.VMEM((2, 7, CROSS_FIRST, block), BF16),
            pltpu.VMEM((2 * tokens, kw), F32),
            pltpu.VMEM((tokens, kw), F32),
            pltpu.VMEM((NZ, 2, tokens, block), BF16),
            dma((4,)),
            dma((NZ, 2)),
            dma((1,)),
            dma((NZ, 2)),
            dma((3,)),
            dma((3,)),
            dma((1,)),
            dma((GROUPS,)),
            dma((1,)),
            dma((GROUPS,)),
            dma((1,)),
            dma((NZ,)),
            dma((1,)),
            dma((NZ, NX)),
            dma((1,)),
            dma((NZ, 2)),
            dma((1,)),
            dma((NZ, 2)),
            dma((1,)),
            dma((2, 7, 2)),
            dma((1,)),
            dma((2,)),
            dma((1,)),
            dma((NZ,)),
            dma((1,)),
            dma((2, 7)),
            dma((1,)),
            dma((1,)),
        ],
        compiler_params=pltpu.CompilerParams(
            collective_id=0, has_side_effects=True, vmem_limit_bytes=44 * 2**20
        ),
        cost_estimate=pl.CostEstimate(
            flops=6 * tokens * width * kw, bytes_accessed=16 * 2**20, transcendentals=0
        ),
    )(*[pltpu.with_memory_space_constraint(a, pltpu.HBM) for a in arguments])
    weights, moved, keys, grads, wgrad = pl.pallas_call(
        finish,
        name="finish",
        out_shape=(
            jax.ShapeDtypeStruct((rows, kw), F32),
            jax.ShapeDtypeStruct((rows, kw), F32),
            jax.ShapeDtypeStruct((tokens, kw), BF16),
            jax.ShapeDtypeStruct((tokens, width), BF16),
            jax.ShapeDtypeStruct((rows, kw), F32),
        ),
        in_specs=[vmem] * 5,
        out_specs=(hbm,) * 5,
        scratch_shapes=[pltpu.VMEM((rows, kw), F32), dma((8,))],
        compiler_params=pltpu.CompilerParams(vmem_limit_bytes=16 * 2**20),
    )(*[pltpu.with_memory_space_constraint(r, pltpu.VMEM) for r in results])
    return weights, moved, keys, grads, wgrad[None]


def solution(mesh):
    placed = (
        P("group", "fsdp", None),
        P("fsdp", None),
        P("fsdp", None),
        P(("group", "fsdp"), None),
        P(("group", "fsdp"), None),
    )
    return jax.shard_map(
        body,
        mesh=mesh,
        in_specs=placed,
        out_specs=(
            P("fsdp", None),
            P("fsdp", None),
            P(("group", "fsdp"), None),
            P(("group", "fsdp"), None),
            P("group", "fsdp", None),
        ),
        check_vma=False,
    )
```
